128 devices in a mesh: chan: 16 (over y_lo, z, core), lag: 8 (over y_hi, x).
Axes of the slice: x: 4, y: 4 (y_hi: 2, y_lo: 2; y = y_hi * 2 + y_lo), z: 4, core: 2. Of those that a mesh axis runs over, the one named last changes fastest.
Arguments:
- raw: bfloat16 [4096, 40000], P('chan', 'lag'), may hold values from -720 to 720
- fir_taps: bfloat16 [80], replicated, may hold values from -0.625 to 0.625
- channel_map: int32 [4096], P('chan'), may hold values from 0 to 4095, as said below
- lag_offsets: int32 [32], P('lag'), may hold values from -40 to 40, as said below
Outputs:
- correlation: float32 [4096, 32, 4096], P('chan', 'lag')
The draws below stay inside these ranges and needn't reach their ends.
Inputs may be any that keep to these rules, and one draw needn't show every extreme that they name: A permutation of the channels that keeps each channel in its aligned group of 256: channel_map[c] // 256 == c // 256. `lag_offsets`: distinct values; both ends of the range are taken.
All inputs are finite; a program needn't handle non-finite values.
Results may differ from the reference program's by a relative error of at most 0.004.
Values may be sent and summed in bfloat16 or wider, within the bound.
A program may use at most 256 MiB of HBM per device.

```python
import math
import jax
import jax.numpy as jnp
from jax import lax

CB = 256
SAMPLES = 2000
DEC = 20
TAPS = 80
MAXLAG = 40
CHANNELS = 4096
LAGS = 32


def draw_raw(key, part):
    key = jax.random.fold_in(key, 1)
    k_scale, k_env, k_off, k_noise = jax.random.split(key, 4)
    spread = math.log(10.0)
    noise = jnp.clip(jax.random.normal(k_noise, (CHANNELS, DEC * SAMPLES), jnp.float32), -6.0, 6.0)
    scales = jnp.exp(spread * jax.random.uniform(k_scale, (CHANNELS, 1), jnp.float32))
    envelope = jnp.exp(math.log(3.0) * jax.random.uniform(k_env, (1, SAMPLES // 8), jnp.float32))
    envelope = jnp.repeat(envelope, DEC * 8, axis=1)
    offsets = 2.0 * jnp.clip(jax.random.normal(k_off, (CHANNELS, 1), jnp.float32), -3.0, 3.0)
    return (scales * (envelope * noise + offsets)).astype(jnp.bfloat16)


def draw_channel_map(key, part):
    key = jax.random.fold_in(key, 2)
    group_keys = jax.random.split(key, CHANNELS // CB)

    def group_perm(subkey):
        return jax.random.permutation(subkey, CB).astype(jnp.int32)
    local_perm = jax.vmap(group_perm)(group_keys)
    bases = jnp.arange(CHANNELS // CB, dtype=jnp.int32)[:, None] * CB
    return (local_perm + bases).reshape(CHANNELS).astype(jnp.int32)


def draw_lag_offsets(key, part):
    key = jax.random.fold_in(key, 3)
    k_inner, k_place = jax.random.split(key, 2)
    inner = jax.random.permutation(k_inner, 2 * MAXLAG - 1).astype(jnp.int32) - (MAXLAG - 1)
    values = jnp.concatenate([jnp.array([-MAXLAG, MAXLAG], jnp.int32), inner[:LAGS - 2]])
    placing = jax.random.permutation(k_place, LAGS)
    return values[placing].astype(jnp.int32)


def scatter_about(rng, extent, scale, limit, kind=jnp.bfloat16):
    result = jax.random.normal(rng, extent, jnp.float32) * scale
    return jnp.minimum(jnp.maximum(result, -limit), limit).astype(kind)


def setup_inputs(seed: int = 0) -> dict:
    streams_of = jax.random.split(jax.random.key(seed), 5)
    raw = draw_raw(jax.random.fold_in(streams_of[4], 71), 0)
    fir_taps = scatter_about(streams_of[1], (TAPS,), TAPS ** -0.5, 0.625)
    channel_map = draw_channel_map(jax.random.fold_in(streams_of[4], 71), 0)
    lag_offsets = draw_lag_offsets(jax.random.fold_in(streams_of[4], 71), 0)
    return {"raw": raw, "fir_taps": fir_taps, "channel_map": channel_map, "lag_offsets": lag_offsets}


def decimate(series, fir_taps):
    lead_cols = jnp.zeros((series.shape[0], TAPS - DEC), jnp.float32)
    joined = jnp.concatenate([lead_cols, series.astype(jnp.float32)], axis=1)
    blocks = joined.reshape(joined.shape[0], -1, DEC)
    tap_table = fir_taps[::-1].astype(jnp.float32).reshape(TAPS // DEC, DEC)
    out_len = series.shape[1] // DEC
    summed = jnp.zeros((series.shape[0], out_len), jnp.float32)
    for index in range(TAPS // DEC):
        summed = summed + jnp.einsum('cnr,r->cn', blocks[:, index:index + out_len, :], tap_table[index], precision=lax.Precision.HIGHEST)
    return summed

def whiten(decimated):
    average = lax.optimization_barrier(jnp.mean(decimated, axis=1, keepdims=True))
    centred = decimated - average
    energy = lax.optimization_barrier(jnp.mean(centred * centred, axis=1, keepdims=True))
    return (centred * lax.rsqrt(energy + 1e-05)).astype(jnp.bfloat16)

def reference(raw, fir_taps, channel_map, lag_offsets):
    whitened = whiten(decimate(raw, fir_taps))
    ordered = jnp.zeros_like(whitened).at[channel_map].set(whitened)
    padded = jnp.pad(ordered, ((0, 0), (MAXLAG, MAXLAG)))

    def shift_one(offset):
        return lax.dynamic_slice_in_dim(padded, (offset + MAXLAG).astype(jnp.int32), SAMPLES, 1)
    shifted = jax.vmap(shift_one)(lag_offsets).astype(jnp.float32)
    scale = 1.0 / math.sqrt(SAMPLES)
    row_blocks = ordered.astype(jnp.float32).reshape(CHANNELS // CB, CB, SAMPLES)

    def block_corr(rows_here):
        return jnp.einsum('it,ljt->ilj', rows_here, shifted, precision=lax.Precision.HIGHEST) * scale
    return lax.map(block_corr, row_blocks).reshape(CHANNELS, LAGS, CHANNELS)
```

```python
import functools
import math

import jax
import jax.numpy as jnp
from jax import lax
from jax.experimental import pallas as pl
from jax.experimental.pallas import tpu as pltpu
from jax.sharding import PartitionSpec as P

MESH = pl.DeviceIdType.MESH
DEC = 20
TAPS = 80
MAXLAG = 40
CB = 256
SAMPLES = 2000
CHANNELS = 4096
SLOTS = 4
STEP = 250
HEAD = 3
ROWS = 5000
F32, BF16 = jnp.float32, jnp.bfloat16

EARLY = 12
COPIES = (
    ((0, 0, 1), 2, 0, 256), ((0, 0, 2), 2, 0, 256), ((0, 0, 3), 2, 0, 256), ((0, 1, 0), 1, 0, 256),
    ((0, 1, 1), 1, 0, 80), ((0, 1, 1), 2, 80, 176), ((0, 1, 2), 1, 0, 80), ((0, 1, 2), 2, 80, 176),
    ((0, 1, 3), 1, 0, 80), ((0, 1, 3), 2, 80, 176), ((0, 2, 0), 1, 0, 256), ((0, 2, 1), 1, 0, 80),
    ((0, 2, 1), 2, 80, 176), ((0, 2, 2), 1, 0, 80), ((0, 2, 2), 2, 80, 176), ((0, 2, 3), 1, 0, 80),
    ((0, 2, 3), 2, 80, 176), ((0, 3, 0), 1, 0, 256), ((0, 3, 1), 1, 0, 80), ((0, 3, 1), 2, 80, 176),
    ((0, 3, 2), 1, 0, 80), ((0, 3, 2), 2, 80, 176), ((0, 3, 3), 1, 0, 80), ((0, 3, 3), 2, 80, 176),
    ((1, 0, 0), 0, 0, 256), ((1, 0, 1), 0, 0, 80), ((1, 0, 1), 0, 160, 96), ((1, 0, 1), 2, 80, 80),
    ((1, 0, 2), 0, 0, 80), ((1, 0, 2), 0, 160, 96), ((1, 0, 2), 2, 80, 80), ((1, 0, 3), 0, 0, 80),
    ((1, 0, 3), 0, 160, 96), ((1, 0, 3), 2, 80, 80), ((1, 1, 0), 1, 0, 160), ((1, 1, 0), 0, 160, 96),
    ((1, 1, 1), 1, 0, 80), ((1, 1, 1), 1, 160, 96), ((1, 1, 1), 2, 80, 80), ((1, 1, 2), 1, 0, 80),
    ((1, 1, 2), 2, 80, 80), ((1, 1, 2), 0, 160, 96), ((1, 1, 3), 1, 0, 80), ((1, 1, 3), 2, 80, 80),
    ((1, 1, 3), 0, 160, 96), ((1, 2, 0), 1, 0, 160), ((1, 2, 0), 0, 160, 96), ((1, 2, 1), 1, 0, 80),
    ((1, 2, 1), 2, 80, 176), ((1, 2, 2), 1, 0, 80), ((1, 2, 2), 2, 80, 80), ((1, 2, 2), 0, 160, 96),
    ((1, 2, 3), 1, 0, 80), ((1, 2, 3), 2, 80, 176), ((1, 3, 0), 1, 0, 160), ((1, 3, 0), 0, 160, 96),
    ((1, 3, 1), 1, 0, 80), ((1, 3, 1), 1, 160, 96), ((1, 3, 1), 2, 80, 80), ((1, 3, 2), 1, 0, 80),
    ((1, 3, 2), 2, 80, 80), ((1, 3, 2), 0, 160, 96), ((1, 3, 3), 1, 0, 80), ((1, 3, 3), 2, 80, 80),
    ((1, 3, 3), 0, 160, 96), ((2, 0, 0), 0, 0, 256), ((2, 0, 1), 0, 0, 80), ((2, 0, 1), 0, 160, 96),
    ((2, 0, 1), 2, 80, 80), ((2, 0, 2), 0, 0, 80), ((2, 0, 2), 0, 160, 96), ((2, 0, 2), 2, 80, 80),
    ((2, 0, 3), 0, 0, 80), ((2, 0, 3), 0, 160, 96), ((2, 0, 3), 2, 80, 80), ((2, 1, 0), 1, 0, 160),
    ((2, 1, 0), 0, 160, 96), ((2, 1, 1), 1, 0, 80), ((2, 1, 1), 2, 80, 80), ((2, 1, 1), 0, 160, 96),
    ((2, 1, 2), 1, 0, 80), ((2, 1, 2), 2, 80, 80), ((2, 1, 2), 0, 160, 96), ((2, 1, 3), 1, 0, 80),
    ((2, 1, 3), 2, 80, 80), ((2, 1, 3), 0, 160, 96), ((2, 2, 0), 1, 0, 160), ((2, 2, 0), 0, 160, 96),
    ((2, 2, 1), 1, 0, 80), ((2, 2, 1), 2, 80, 80), ((2, 2, 1), 0, 160, 96), ((2, 2, 2), 1, 0, 80),
    ((2, 2, 2), 2, 80, 80), ((2, 2, 2), 0, 160, 96), ((2, 2, 3), 1, 0, 80), ((2, 2, 3), 2, 80, 80),
    ((2, 2, 3), 0, 160, 96), ((2, 3, 0), 1, 0, 160), ((2, 3, 0), 0, 160, 96), ((2, 3, 1), 1, 0, 80),
    ((2, 3, 1), 2, 80, 80), ((2, 3, 1), 0, 160, 96), ((2, 3, 2), 1, 0, 80), ((2, 3, 2), 2, 80, 80),
    ((2, 3, 2), 0, 160, 96), ((2, 3, 3), 1, 0, 80), ((2, 3, 3), 2, 80, 80), ((2, 3, 3), 0, 160, 96),
    ((3, 0, 0), 0, 0, 256), ((3, 0, 1), 0, 0, 80), ((3, 0, 1), 0, 160, 96), ((3, 0, 1), 2, 80, 80),
    ((3, 0, 2), 0, 0, 80), ((3, 0, 2), 0, 160, 96), ((3, 0, 2), 2, 80, 80), ((3, 0, 3), 0, 0, 80),
    ((3, 0, 3), 0, 160, 96), ((3, 0, 3), 2, 80, 80), ((3, 1, 0), 1, 0, 160), ((3, 1, 0), 0, 160, 96),
    ((3, 1, 1), 1, 0, 80), ((3, 1, 1), 2, 80, 80), ((3, 1, 1), 0, 160, 96), ((3, 1, 2), 1, 0, 80),
    ((3, 1, 2), 2, 80, 80), ((3, 1, 2), 0, 160, 96), ((3, 1, 3), 1, 0, 80), ((3, 1, 3), 2, 80, 80),
    ((3, 1, 3), 0, 160, 96), ((3, 2, 0), 1, 0, 160), ((3, 2, 0), 0, 160, 96), ((3, 2, 1), 1, 0, 80),
    ((3, 2, 1), 2, 80, 80), ((3, 2, 1), 0, 160, 96), ((3, 2, 2), 1, 0, 80), ((3, 2, 2), 2, 80, 80),
    ((3, 2, 2), 0, 160, 96), ((3, 2, 3), 1, 0, 80), ((3, 2, 3), 2, 80, 80), ((3, 2, 3), 0, 160, 96),
    ((3, 3, 0), 1, 0, 160), ((3, 3, 0), 0, 160, 96), ((3, 3, 1), 1, 0, 80), ((3, 3, 1), 2, 80, 80),
    ((3, 3, 1), 0, 160, 96), ((3, 3, 2), 1, 0, 80), ((3, 3, 2), 2, 80, 80), ((3, 3, 2), 0, 160, 96),
    ((3, 3, 3), 1, 0, 80), ((3, 3, 3), 2, 80, 80), ((3, 3, 3), 0, 160, 96),
)
ACTIONS = (
    ("s", 108), ("s", 17), ("s", 0), ("s", 24), ("s", 3), ("s", 2), ("y", (0, 0, 0)), ("w", 108), ("s", 65),
    ("w", 17), ("s", 10), ("s", 19), ("w", 0), ("s", 109), ("s", 140), ("s", 23), ("s", 25), ("y", (0, 0, 1)),
    ("y", (0, 3, 0)), ("y", (3, 0, 0)), ("s", 111), ("s", 141), ("s", 18), ("s", 117), ("s", 118), ("s", 110),
    ("w", 24), ("s", 27), ("w", 3), ("y", (0, 1, 0)), ("y", (1, 0, 0)), ("w", 2), ("y", (0, 0, 3)), ("s", 1),
    ("s", 115), ("s", 54), ("s", 119), ("s", 31), ("w", 65), ("y", (2, 0, 0)), ("s", 97), ("w", 10),
    ("y", (0, 2, 0)), ("s", 12), ("s", 130), ("w", 109), ("s", 66), ("w", 140), ("s", 129), ("s", 5), ("s", 46),
    ("w", 18), ("w", 19), ("y", (0, 3, 1)), ("w", 141), ("y", (3, 3, 0)), ("s", 35), ("w", 25), ("s", 56),
    ("w", 110), ("w", 111), ("y", (3, 0, 1)), ("s", 16), ("s", 142), ("s", 55), ("s", 34), ("w", 115), ("s", 72),
    ("w", 118), ("w", 119), ("y", (3, 1, 0)), ("s", 9), ("s", 76), ("w", 1), ("y", (0, 0, 2)), ("w", 54), ("s", 45),
    ("s", 112), ("s", 68), ("w", 130), ("s", 87), ("w", 97), ("s", 86), ("s", 58), ("w", 12), ("s", 133),
    ("w", 129), ("y", (3, 2, 0)), ("s", 132), ("s", 98), ("w", 66), ("s", 99), ("s", 100), ("s", 75), ("s", 26),
    ("w", 55), ("y", (1, 3, 0)), ("s", 121), ("w", 16), ("s", 14), ("w", 5), ("s", 122), ("w", 34), ("w", 35),
    ("y", (1, 1, 0)), ("s", 11), ("s", 144), ("w", 56), ("s", 47), ("s", 38), ("s", 67), ("w", 45), ("w", 46),
    ("y", (1, 2, 0)), ("w", 142), ("s", 131), ("s", 48), ("s", 116), ("s", 22), ("w", 86), ("w", 87),
    ("y", (2, 2, 0)), ("w", 133), ("s", 90), ("w", 31), ("s", 62), ("L", 0), ("s", 139), ("w", 99), ("s", 88),
    ("s", 89), ("s", 28), ("w", 72), ("s", 105), ("w", 75), ("s", 78), ("w", 112), ("s", 69), ("s", 148),
    ("s", 143), ("w", 122), ("s", 79), ("s", 4), ("w", 9), ("s", 7), ("w", 144), ("s", 101), ("s", 36), ("w", 23),
    ("s", 21), ("s", 128), ("w", 26), ("s", 37), ("s", 57), ("w", 11), ("y", (0, 2, 1)), ("w", 22),
    ("y", (0, 3, 3)), ("w", 27), ("y", (1, 0, 1)), ("w", 48), ("w", 47), ("y", (1, 2, 1)), ("w", 67), ("w", 68),
    ("y", (2, 0, 1)), ("w", 76), ("y", (2, 1, 0)), ("w", 98), ("y", (2, 3, 0)), ("w", 116), ("w", 117),
    ("y", (3, 0, 3)), ("w", 131), ("w", 132), ("y", (3, 2, 1)), ("s", 150), ("s", 77), ("s", 33), ("s", 32),
    ("w", 88), ("w", 89), ("w", 90), ("y", (2, 2, 1)), ("s", 120), ("s", 53), ("C", 0), ("s", 73), ("s", 15),
    ("s", 74), ("w", 139), ("s", 96), ("w", 62), ("s", 52), ("s", 95), ("s", 113), ("w", 105), ("s", 94), ("w", 4),
    ("y", (0, 1, 1)), ("w", 143), ("y", (3, 3, 1)), ("w", 148), ("s", 137), ("w", 100), ("w", 101),
    ("y", (2, 3, 1)), ("w", 14), ("s", 136), ("s", 138), ("D", 0), ("s", 44), ("s", 20), ("s", 43), ("s", 64),
    ("w", 28), ("s", 59), ("s", 63), ("w", 128), ("s", 85), ("w", 69), ("s", 102), ("s", 84), ("s", 145),
    ("s", 106), ("w", 32), ("w", 33), ("y", (1, 0, 3)), ("w", 36), ("w", 37), ("w", 38), ("y", (1, 1, 1)),
    ("w", 57), ("w", 58), ("y", (1, 3, 1)), ("w", 77), ("w", 78), ("w", 79), ("y", (2, 1, 1)), ("w", 120),
    ("w", 121), ("y", (3, 1, 1)), ("w", 150), ("s", 107), ("s", 8), ("s", 127), ("w", 15), ("y", (0, 2, 3)),
    ("w", 52), ("w", 53), ("y", (1, 2, 3)), ("s", 42), ("w", 7), ("s", 125), ("s", 149), ("w", 73), ("w", 74),
    ("y", (2, 0, 3)), ("C", 1), ("w", 21), ("s", 147), ("s", 83), ("s", 30), ("s", 29), ("s", 126), ("s", 50),
    ("s", 51), ("w", 20), ("s", 13), ("s", 71), ("w", 59), ("s", 49), ("w", 95), ("s", 92), ("y", (0, 3, 2)),
    ("w", 96), ("w", 94), ("y", (2, 2, 3)), ("w", 137), ("w", 138), ("y", (3, 2, 3)), ("w", 113), ("s", 70),
    ("w", 102), ("s", 91), ("s", 114), ("w", 64), ("w", 63), ("y", (1, 3, 3)), ("D", 1), ("w", 136), ("s", 93),
    ("w", 145), ("s", 134), ("s", 135), ("s", 41), ("s", 6), ("w", 43), ("s", 40), ("s", 61), ("s", 39), ("s", 60),
    ("s", 80), ("w", 84), ("s", 81), ("w", 8), ("y", (0, 1, 3)), ("w", 42), ("w", 44), ("y", (1, 1, 3)), ("w", 83),
    ("w", 85), ("y", (2, 1, 3)), ("w", 106), ("w", 107), ("y", (2, 3, 3)), ("w", 126), ("w", 127), ("y", (3, 1, 3)),
    ("w", 149), ("y", (3, 3, 3)), ("w", 125), ("s", 82), ("s", 123), ("s", 103), ("w", 29), ("w", 30),
    ("y", (1, 0, 2)), ("w", 147), ("s", 104), ("w", 13), ("y", (0, 2, 2)), ("s", 124), ("C", 2), ("s", 146),
    ("w", 49), ("w", 50), ("w", 51), ("y", (1, 2, 2)), ("w", 70), ("w", 71), ("y", (2, 0, 2)), ("w", 91), ("w", 92),
    ("w", 93), ("y", (2, 2, 2)), ("w", 114), ("y", (3, 0, 2)), ("w", 134), ("w", 135), ("y", (3, 2, 2)), ("w", 6),
    ("y", (0, 1, 2)), ("D", 2), ("w", 40), ("w", 41), ("w", 39), ("y", (1, 1, 2)), ("w", 60), ("w", 61),
    ("y", (1, 3, 2)), ("w", 80), ("w", 81), ("w", 82), ("y", (2, 1, 2)), ("C", 3), ("w", 104), ("w", 103),
    ("y", (2, 3, 2)), ("w", 123), ("w", 124), ("y", (3, 1, 2)), ("w", 146), ("y", (3, 3, 2)), ("D", 3), ("C", 4),
    ("D", 4), ("C", 5), ("D", 5),
)


def dims():
    chan, lag = lax.axis_index("chan"), lax.axis_index("lag")
    core, z, y_lo = chan % 2, (chan // 2) % 4, chan // 8
    x, y = lag % 4, (lag // 4) * 2 + y_lo
    return x, y, z, core


def device(x, y, z, core):
    return (((y % 2) * 4 + z) * 2 + core, (y // 2) * 4 + x)


def group_channels(coords, group, other):
    _, y, z, core = coords
    ahead = 1 - 2 * core
    sign = -ahead if other else ahead
    z_there = (z + 4 + sign * (0, 1, -1, 2)[group // 2]) % 4
    core_there = 1 - core if other else core
    return (((y + group) % 2) * 4 + z_there) * 2 + core_there


def multiply(lhs_ref, g_ref, channels):
    block = g_ref[pl.ds(channels * 8, 8)].reshape(8 * CB, CB)
    product = jnp.dot(lhs_ref[...], block, preferred_element_type=F32)
    return (product * (1.0 / math.sqrt(SAMPLES))).reshape(CB, SLOTS, CB)


def gather_kernel(
    raw_hbm, taps_ref, map_ref, lags_ref, part_ref, lhs_ref, g_ref,
    raw_ref, dec_ref, stat_ref, turned_ref, shift_ref, mixed_ref,
    raw_sem, stat_send, stat_recv, send_sem, recv_sem, other_send, other_recv,
):
    coords = x, y, z, core = dims()
    me, lag = device(*coords)
    ahead = 1 - 2 * core

    raw_copy = pltpu.make_async_copy(raw_hbm, raw_ref, raw_sem)
    raw_copy.start()

    def lag_peer(step):
        return me, (lag + step) % 8

    sibling = device(x, y, z, 1 - core)
    barrier = pltpu.get_barrier_semaphore()
    peers = [lag_peer(step) for step in range(1, 8)] + [sibling]
    peers += [device(x, (y + step) % 4, z, core) for step in (1, 3)]
    peers += [device(x, y, (z + step) % 4, core) for step in (1, 3)]
    for peer in peers:
        pl.semaphore_signal(barrier, inc=1, device_id=peer, device_id_type=MESH)

    taps = jnp.broadcast_to(taps_ref[...].astype(F32), (8, TAPS)).astype(BF16)
    spread = lax.broadcasted_iota(jnp.int32, (TAPS, 256), 0) + lax.broadcasted_iota(jnp.int32, (TAPS, 256), 1)
    spread = (spread == 128 + DEC - 1).astype(F32).astype(BF16)
    first = jnp.dot(taps, spread, preferred_element_type=F32)
    first = jnp.concatenate([first, jnp.zeros((8, 512), F32)], axis=1)
    wide = lax.broadcasted_iota(jnp.int32, (8, 768), 0)
    band = first
    for step in range(1, 8):
        band = jnp.where(wide == step, pltpu.roll(first, DEC * step, 1), band)
    band = jnp.concatenate([band] + [pltpu.roll(band, 8 * DEC * step, 1) for step in range(1, 4)], axis=0)
    next_band = pltpu.roll(band[0:16, 0:256], 8, 1).astype(BF16)
    band = band.astype(BF16)

    row = lax.broadcasted_iota(jnp.int32, (512, 256), 0)
    far = 10000
    time = jnp.where(
        row < 256,
        jnp.where(row < STEP, row, far),
        jnp.where(row < 384, jnp.where(row - 128 < STEP, row - 128 - STEP, far), row - 384 + STEP),
    )
    column = lax.broadcasted_iota(jnp.int32, (512, 256), 1)
    column = jnp.where(column < STEP, column, -far)
    time = time - column
    for slot in range(SLOTS):
        shift_ref[slot] = (time == -lags_ref[slot]).astype(F32).astype(BF16)

    raw_copy.wait()
    tail = jnp.concatenate([raw_ref[4992:5000].astype(F32), jnp.zeros((8, CB), F32)], axis=0).astype(BF16)
    blank = jnp.zeros((112, CB), BF16)
    window = jnp.concatenate([raw_ref[4864:4992], tail, blank], axis=0)
    over = jnp.dot(next_band, window, preferred_element_type=F32)[0:8]
    for part in range(8):
        begin = 640 * part - 128
        if part == 0:
            piece = jnp.dot(band[:, 128:], raw_ref[0:640], preferred_element_type=F32)
        elif part == 7:
            window = jnp.concatenate([raw_ref[begin:4992], tail, blank], axis=0)
            piece = jnp.dot(band, window, preferred_element_type=F32)
        else:
            piece = jnp.dot(band, raw_ref[begin : begin + 768], preferred_element_type=F32)
        dec_ref[32 * part : 32 * part + 32] = piece

    dec = dec_ref[...]
    sample = lax.broadcasted_iota(jnp.int32, (CB, CB), 0)
    whole = (sample >= HEAD) & (sample < STEP)
    count = STEP - HEAD
    mean = jnp.sum(jnp.where(whole, dec, 0.0), axis=0, keepdims=True) * (1.0 / count)
    spread2 = jnp.where(whole, dec - mean, 0.0)
    energy = jnp.sum(spread2 * spread2, axis=0, keepdims=True)
    line = lax.broadcasted_iota(jnp.int32, (8, CB), 0)
    stat_ref[lag] = jnp.where(
        line == 0,
        mean,
        jnp.where(
            line == 1,
            energy,
            jnp.where(line < 5, pltpu.roll(dec[0:8], 2, 0), pltpu.roll(over, 5, 0)),
        ),
    )
    pl.semaphore_wait(barrier, len(peers))

    def stat_copy(step):
        return pltpu.make_async_remote_copy(
            src_ref=stat_ref.at[lag],
            dst_ref=stat_ref.at[lag],
            send_sem=stat_send.at[step],
            recv_sem=stat_recv.at[step],
            device_id=lag_peer(step),
            device_id_type=MESH,
        )

    for step in range(1, 8):
        stat_copy(step).start()
    order = lax.broadcasted_iota(jnp.int32, (CB, CB), 0)
    place = (map_ref[...] - (me * CB) == order).astype(F32).astype(BF16)
    for step in range(1, 8):
        stat_copy(step).wait_recv()

    stats = [stat_ref[d] for d in range(8)]
    total = jnp.zeros((8, CB), F32)
    heads = []
    before = jnp.zeros((8, CB), F32)
    for d in range(8):
        head = pltpu.roll(stats[d], 6, 0)
        if d:
            from_left = pltpu.roll(stats[d - 1], 3, 0)
            head = head + from_left
            before = before + jnp.where(lag == d, from_left, 0.0)
        heads.append(head)
        total = total + jnp.where(line < HEAD, head, 0.0)
    mean = count * sum(s[0:1] for s in stats) + jnp.sum(total, axis=0, keepdims=True)
    mean = mean * (1.0 / SAMPLES)
    energy = jnp.zeros((1, CB), F32)
    total = jnp.zeros((8, CB), F32)
    for d in range(8):
        away = stats[d][0:1] - mean
        energy = energy + stats[d][1:2] + count * (away * away)
        away = jnp.where(line < HEAD, heads[d] - mean, 0.0)
        total = total + away * away
    energy = (energy + jnp.sum(total, axis=0, keepdims=True)) * (1.0 / SAMPLES)
    scale = lax.rsqrt(energy + 1e-05)
    dec_ref[0:8] = dec_ref[0:8] + jnp.where(line < HEAD, before, 0.0)
    white = jnp.where(sample < STEP, (dec_ref[...] - mean) * scale, 0.0).astype(BF16)
    ordered = lax.dot_general(white, place, (((1,), (1,)), ((), ())), preferred_element_type=F32)

    there = (0, 1, 2, -1)
    at_x = [(x + 4 + ahead * k) % 4 for k in there]
    at_y = [(y + 4 + ahead * k) % 4 for k in there]
    at_z = [(z + 4 + ahead * k) % 4 for k in there]
    term_y = [(k % 2) * 64 + (k // 2) * 4 for k in at_y]
    term_z = [k * 16 + core * 8 for k in at_z]

    def place_of(offset):
        return at_x[offset[0]] + term_y[offset[1]] + term_z[offset[2]]

    neighbours = {}
    for step in (1, 3):
        neighbours[0, step] = device(at_x[step], y, z, core)
        neighbours[1, step] = device(x, at_y[step], z, core)
        neighbours[2, step] = device(x, y, at_z[step], core)

    g_ref[place_of((0, 0, 0))] = ordered.astype(BF16)

    def block_copy(index):
        offset, axis, row, rows = COPIES[index]
        sent = list(offset)
        sent[axis] = {1: 0, 3: 0, 2: 3}[offset[axis]]
        to = 3 if offset[axis] == 1 else 1
        here = g_ref.at[place_of(sent), pl.ds(row, rows)]
        return pltpu.make_async_remote_copy(
            src_ref=here, dst_ref=here, send_sem=send_sem, recv_sem=recv_sem.at[index],
            device_id=neighbours[axis, to], device_id_type=MESH,
        )

    def block_wait(index):
        offset, axis, row, rows = COPIES[index]
        here = g_ref.at[place_of(offset), pl.ds(row, rows)]
        pltpu.make_async_copy(here, here, recv_sem.at[index]).wait()

    def hand_over(offset):
        here = g_ref.at[place_of(offset)]
        group = (at_y[offset[1]] % 2) * 4 + at_z[offset[2]]
        pltpu.make_async_remote_copy(
            src_ref=here, dst_ref=here, send_sem=other_send, recv_sem=other_recv.at[group],
            device_id=sibling, device_id_type=MESH,
        ).start()

    def taken_over(group):
        channels = group_channels(coords, group, True)
        here = g_ref.at[pl.ds(channels * 8, 8)]
        pltpu.make_async_copy(here, here, other_recv.at[channels // 2]).wait()

    def build_own():
        eye = lax.broadcasted_iota(jnp.int32, (CB, CB), 0) == lax.broadcasted_iota(jnp.int32, (CB, CB), 1)
        eye = eye.astype(F32).astype(BF16)
        turned_ref[0] = jnp.zeros((CB, CB), BF16)
        turned_ref[9] = jnp.zeros((CB, CB), BF16)

        def turn(d, carry):
            turned = lax.dot_general(eye, g_ref[me * 8 + d], (((1,), (1,)), ((), ())), preferred_element_type=F32)
            turned_ref[d + 1] = turned.astype(BF16)
            return carry

        lax.fori_loop(0, 8, turn, 0)

        def shift(d, carry):
            around = jnp.concatenate(
                [turned_ref[d + 1], turned_ref[d, :, 128:256], turned_ref[d + 2, :, 0:128]], axis=1
            )
            for slot in range(SLOTS):
                moved = jnp.dot(around, shift_ref[slot], preferred_element_type=F32)
                for half in range(2):
                    mixed_ref[half, pl.ds(slot, CB, stride=SLOTS), :] = moved[:, 128 * half : 128 * half + 128]
            for half in range(2):
                there = pl.ds(pl.multiple_of(d * CB + 128 * half, 128), 128)
                lhs_ref[:, there] = mixed_ref[half].astype(BF16)
            return carry

        lax.fori_loop(0, 8, shift, 0)

    for kind, what in ACTIONS:
        if kind == "w":
            block_wait(what)
        elif kind == "s":
            block_copy(what).start()
        elif kind == "y":
            hand_over(what)
        elif kind == "L":
            build_own()
        elif kind == "C":
            part_ref[2 * what] = multiply(lhs_ref, g_ref, group_channels(coords, what, False))
        elif kind == "D":
            taken_over(what)
            part_ref[2 * what + 1] = multiply(lhs_ref, g_ref, group_channels(coords, what, True))
    for group in range(EARLY // 2, 8):
        taken_over(group)

    for step in range(1, 8):
        stat_copy(step).wait_send()
    gone = g_ref.at[pl.ds(0, 63)]
    pltpu.make_async_copy(gone, gone, send_sem).wait()
    gone = g_ref.at[pl.ds(0, 64)]
    pltpu.make_async_copy(gone, gone, other_send).wait()


def finish_kernel(part_ref, lhs_ref, g_ref, out_ref, stage_ref, part_sem, stage_sem):
    coords = dims()
    late = 16 - EARLY

    def columns(group, other):
        channels = group_channels(coords, group, other)
        return out_ref.at[:, :, pl.ds(pl.multiple_of(channels * CB, CB), CB)]

    def early_copy(index):
        return pltpu.make_async_copy(part_ref.at[index], columns(index // 2, index % 2), part_sem.at[index])

    def late_copy(index):
        there = columns((EARLY + index) // 2, index % 2)
        return pltpu.make_async_copy(stage_ref.at[index], there, stage_sem.at[index])

    for index in range(EARLY):
        early_copy(index).start()
    for index in range(late):
        channels = group_channels(coords, (EARLY + index) // 2, index % 2)
        stage_ref[index] = multiply(lhs_ref, g_ref, channels)
        late_copy(index).start()
    for index in range(EARLY):
        early_copy(index).wait()
    for index in range(late):
        late_copy(index).wait()


def local(raw, fir_taps, channel_map, lag_offsets):
    vmem = pl.BlockSpec(memory_space=pltpu.VMEM)
    part, lhs, blocks = pl.pallas_call(
        gather_kernel,
        out_shape=[
            pltpu.VMEM((EARLY, CB, SLOTS, CB), F32),
            pltpu.VMEM((CB * SLOTS, 8 * CB), BF16),
            pltpu.VMEM((128, CB, CB), BF16),
        ],
        in_specs=[pl.BlockSpec(memory_space=pltpu.HBM), vmem, vmem, pl.BlockSpec(memory_space=pltpu.SMEM)],
        out_specs=[vmem] * 3,
        scratch_shapes=[
            pltpu.VMEM((ROWS, CB), BF16),
            pltpu.VMEM((CB, CB), F32),
            pltpu.VMEM((8, 8, CB), F32),
            pltpu.VMEM((10, CB, CB), BF16),
            pltpu.VMEM((SLOTS, 512, CB), BF16),
            pltpu.VMEM((2, CB * SLOTS, 128), F32),
            pltpu.SemaphoreType.DMA,
            pltpu.SemaphoreType.DMA((8,)),
            pltpu.SemaphoreType.DMA((8,)),
            pltpu.SemaphoreType.DMA,
            pltpu.SemaphoreType.DMA((len(COPIES),)),
            pltpu.SemaphoreType.DMA,
            pltpu.SemaphoreType.DMA((8,)),
        ],
        compiler_params=pltpu.CompilerParams(collective_id=0, has_side_effects=True, vmem_limit_bytes=14 << 20),
        name="gather",
    )(raw.T, fir_taps.reshape(1, TAPS), channel_map.reshape(1, CB), lag_offsets)
    part, lhs, blocks = [pltpu.with_memory_space_constraint(a, pltpu.VMEM) for a in (part, lhs, blocks)]
    return pl.pallas_call(
        finish_kernel,
        out_shape=jax.ShapeDtypeStruct((CB, SLOTS, CHANNELS), F32),
        in_specs=[vmem] * 3,
        out_specs=pl.BlockSpec(memory_space=pltpu.HBM),
        scratch_shapes=[
            pltpu.VMEM((16 - EARLY, CB, SLOTS, CB), F32),
            pltpu.SemaphoreType.DMA((EARLY,)),
            pltpu.SemaphoreType.DMA((16 - EARLY,)),
        ],
        compiler_params=pltpu.CompilerParams(vmem_limit_bytes=(17 - EARLY + 2) << 20),
        name="finish",
    )(part, lhs, blocks)


def solution(mesh):
    placed = (P("chan", "lag"), P(), P("chan"), P("lag"))
    return jax.shard_map(
        local, mesh=mesh, in_specs=placed, out_specs=P("chan", "lag", None), check_vma=False
    )
```

```python
import functools
import math

import jax
import jax.numpy as jnp
from jax import lax
from jax.experimental import pallas as pl
from jax.experimental.pallas import tpu as pltpu
from jax.sharding import PartitionSpec as P

MESH = pl.DeviceIdType.MESH
DEC = 20
TAPS = 80
MAXLAG = 40
CB = 256
SAMPLES = 2000
CHANNELS = 4096
SLOTS = 4
STEP = 250
HEAD = 3
ROWS = 5000
F32, BF16 = jnp.float32, jnp.bfloat16

EARLY = 12
COPIES = (
    ((0, 0, 1), 2, 0, 256), ((0, 0, 2), 2, 0, 256), ((0, 0, 3), 2, 0, 256), ((0, 1, 0), 1, 0, 256),
    ((0, 1, 1), 2, 0, 256), ((0, 1, 2), 2, 0, 256), ((0, 1, 3), 2, 0, 256), ((0, 2, 0), 1, 0, 256),
    ((0, 2, 1), 1, 0, 256), ((0, 2, 2), 2, 0, 256), ((0, 2, 3), 1, 0, 256), ((0, 3, 0), 1, 0, 256),
    ((0, 3, 1), 2, 0, 256), ((0, 3, 2), 1, 0, 256), ((0, 3, 3), 2, 0, 80), ((0, 3, 3), 2, 160, 96),
    ((0, 3, 3), 1, 80, 80), ((1, 0, 0), 0, 0, 256), ((1, 0, 1), 0, 0, 160), ((1, 0, 1), 2, 160, 96),
    ((1, 0, 2), 2, 0, 256), ((1, 0, 3), 2, 0, 256), ((1, 1, 0), 1, 0, 80), ((1, 1, 0), 0, 80, 176),
    ((1, 1, 1), 1, 0, 256), ((1, 1, 2), 2, 0, 256), ((1, 1, 3), 0, 0, 256), ((1, 2, 0), 1, 0, 160),
    ((1, 2, 0), 0, 160, 96), ((1, 2, 1), 1, 0, 256), ((1, 2, 2), 0, 0, 256), ((1, 2, 3), 1, 0, 256),
    ((1, 3, 0), 1, 0, 160), ((1, 3, 0), 0, 160, 96), ((1, 3, 1), 2, 0, 256), ((1, 3, 2), 2, 0, 256),
    ((1, 3, 3), 0, 0, 256), ((2, 0, 0), 0, 0, 256), ((2, 0, 1), 2, 0, 256), ((2, 0, 2), 2, 0, 256),
    ((2, 0, 3), 0, 0, 256), ((2, 1, 0), 1, 0, 256), ((2, 1, 1), 0, 0, 256), ((2, 1, 2), 1, 0, 256),
    ((2, 1, 3), 0, 0, 256), ((2, 2, 0), 1, 0, 160), ((2, 2, 0), 0, 160, 96), ((2, 2, 1), 2, 0, 256),
    ((2, 2, 2), 1, 0, 256), ((2, 2, 3), 0, 0, 256), ((2, 3, 0), 1, 0, 256), ((2, 3, 1), 2, 0, 256),
    ((2, 3, 2), 1, 0, 256), ((2, 3, 3), 1, 0, 256), ((3, 0, 0), 0, 0, 256), ((3, 0, 1), 0, 0, 256),
    ((3, 0, 2), 0, 0, 256), ((3, 0, 3), 2, 0, 160), ((3, 0, 3), 0, 160, 96), ((3, 1, 0), 0, 0, 256),
    ((3, 1, 1), 2, 0, 256), ((3, 1, 2), 2, 0, 256), ((3, 1, 3), 1, 0, 256), ((3, 2, 0), 1, 0, 160),
    ((3, 2, 0), 0, 160, 96), ((3, 2, 1), 0, 0, 256), ((3, 2, 2), 1, 0, 256), ((3, 2, 3), 0, 0, 256),
    ((3, 3, 0), 0, 0, 256), ((3, 3, 1), 0, 0, 256), ((3, 3, 2), 0, 0, 256), ((3, 3, 3), 1, 0, 256),
)
ACTIONS = (
    ("s", 54), ("s", 11), ("s", 2), ("y", (0, 0, 0)), ("s", 17), ("s", 3), ("s", 0), ("w", 54), ("s", 37),
    ("w", 11), ("s", 7), ("s", 12), ("w", 2), ("y", (0, 0, 3)), ("y", (0, 3, 0)), ("y", (3, 0, 0)), ("s", 68),
    ("s", 16), ("s", 14), ("s", 15), ("w", 17), ("s", 32), ("s", 57), ("w", 0), ("y", (0, 0, 1)), ("w", 3),
    ("y", (0, 1, 0)), ("y", (1, 0, 0)), ("s", 22), ("s", 33), ("s", 19), ("s", 59), ("s", 1), ("w", 37), ("s", 50),
    ("w", 7), ("y", (0, 2, 0)), ("w", 12), ("y", (0, 3, 1)), ("y", (2, 0, 0)), ("s", 8), ("s", 64), ("s", 38),
    ("s", 28), ("w", 16), ("w", 14), ("w", 15), ("y", (0, 3, 3)), ("w", 68), ("y", (3, 3, 0)), ("s", 58), ("w", 32),
    ("s", 27), ("w", 33), ("y", (1, 3, 0)), ("s", 23), ("s", 34), ("s", 63), ("s", 18), ("w", 50), ("y", (2, 3, 0)),
    ("w", 59), ("y", (3, 1, 0)), ("s", 45), ("s", 60), ("w", 1), ("y", (0, 0, 2)), ("w", 64), ("s", 46), ("s", 55),
    ("s", 41), ("w", 8), ("y", (0, 2, 1)), ("w", 57), ("w", 58), ("y", (3, 0, 3)), ("s", 4), ("w", 38),
    ("y", (2, 0, 1)), ("w", 27), ("w", 28), ("y", (1, 2, 0)), ("s", 65), ("s", 10), ("w", 22), ("w", 23),
    ("y", (1, 1, 0)), ("w", 63), ("y", (3, 2, 0)), ("s", 51), ("w", 34), ("y", (1, 3, 1)), ("w", 18), ("w", 19),
    ("y", (1, 0, 1)), ("s", 40), ("s", 29), ("w", 45), ("w", 46), ("y", (2, 2, 0)), ("L", 0), ("s", 36), ("s", 24),
    ("s", 47), ("w", 4), ("y", (0, 1, 1)), ("w", 10), ("y", (0, 2, 3)), ("w", 29), ("y", (1, 2, 1)), ("w", 40),
    ("y", (2, 0, 3)), ("w", 41), ("y", (2, 1, 0)), ("w", 51), ("y", (2, 3, 1)), ("w", 55), ("y", (3, 0, 1)),
    ("w", 60), ("y", (3, 1, 1)), ("w", 65), ("y", (3, 2, 1)), ("s", 67), ("s", 13), ("s", 39), ("C", 0), ("s", 42),
    ("s", 62), ("s", 6), ("D", 0), ("C", 1), ("s", 69), ("w", 36), ("s", 31), ("s", 21), ("w", 24),
    ("y", (1, 1, 1)), ("y", (1, 3, 3)), ("w", 47), ("y", (2, 2, 1)), ("D", 1), ("w", 67), ("s", 49), ("w", 39),
    ("s", 52), ("s", 9), ("w", 13), ("y", (0, 3, 2)), ("y", (2, 0, 2)), ("y", (3, 2, 3)), ("C", 2), ("s", 70),
    ("s", 53), ("w", 6), ("s", 5), ("y", (0, 1, 3)), ("w", 42), ("y", (2, 1, 1)), ("w", 62), ("y", (3, 1, 3)),
    ("D", 2), ("s", 26), ("s", 71), ("w", 21), ("s", 20), ("y", (1, 0, 3)), ("w", 31), ("y", (1, 2, 3)), ("w", 69),
    ("y", (3, 3, 1)), ("C", 3), ("s", 44), ("w", 52), ("s", 48), ("s", 35), ("w", 9), ("y", (0, 2, 2)), ("w", 49),
    ("y", (2, 2, 3)), ("y", (2, 3, 2)), ("D", 3), ("s", 30), ("w", 70), ("s", 66), ("s", 61), ("w", 5),
    ("y", (0, 1, 2)), ("w", 53), ("y", (2, 3, 3)), ("y", (3, 3, 2)), ("C", 4), ("s", 56), ("s", 43), ("w", 26),
    ("s", 25), ("w", 20), ("y", (1, 0, 2)), ("y", (1, 1, 3)), ("w", 71), ("y", (3, 3, 3)), ("D", 4), ("w", 35),
    ("y", (1, 3, 2)), ("w", 44), ("y", (2, 1, 3)), ("w", 48), ("y", (2, 2, 2)), ("C", 5), ("w", 30),
    ("y", (1, 2, 2)), ("w", 61), ("y", (3, 1, 2)), ("w", 66), ("y", (3, 2, 2)), ("D", 5), ("w", 25),
    ("y", (1, 1, 2)), ("w", 43), ("y", (2, 1, 2)), ("w", 56), ("y", (3, 0, 2)),
)

PRODUCTS = [(what, int(kind == "D")) for kind, what in ACTIONS if kind in ("C", "D")]
LATE = [(group, other) for group in range(EARLY // 2, 8) for other in range(2)]


def digits(values, bits):
    return sum(value << (bits * index) for index, value in enumerate(values))


def digit(packed, index, bits):
    return lax.shift_right_logical(jnp.int32(packed), index * bits) & ((1 << bits) - 1)


def pick(products, index):
    group = digit(digits([g % 2 for g, _ in products], 1), index, 1)
    group += 2 * digit(digits([g // 2 for g, _ in products], 2), index, 2)
    return group, digit(digits([o for _, o in products], 1), index, 1)


def dims():
    chan, lag = lax.axis_index("chan"), lax.axis_index("lag")
    core, z, y_lo = chan % 2, (chan // 2) % 4, chan // 8
    x, y = lag % 4, (lag // 4) * 2 + y_lo
    return x, y, z, core


def device(x, y, z, core):
    return (((y % 2) * 4 + z) * 2 + core, (y // 2) * 4 + x)


def group_channels(coords, group, other):
    _, y, z, core = coords
    sign = (1 - 2 * core) * (1 - 2 * other)
    step = group // 2
    step = step + (step // 2) * (5 - 2 * step)
    z_there = (z + 4 + sign * (step - 4 * (step // 3))) % 4
    core_there = core + other - 2 * core * other
    return (((y + group) % 2) * 4 + z_there) * 2 + core_there


def multiply(lhs_ref, g_ref, channels):
    block = g_ref[pl.ds(channels * 8, 8)].reshape(8 * CB, CB)
    product = jnp.dot(lhs_ref[...], block, preferred_element_type=F32)
    return (product * (1.0 / math.sqrt(SAMPLES))).reshape(CB, SLOTS, CB)


def gather_kernel(
    raw_hbm, taps_hbm, map_hbm, lags_hbm, part_ref, lhs_ref, g_ref,
    raw_ref, taps_ref, map_ref, lags_ref, dec_ref, stat_ref, turned_ref, shift_ref, mixed_ref,
    raw_sem, small_sem, stat_send, stat_recv, send_sem, recv_sem, other_send, other_recv,
):
    coords = x, y, z, core = dims()
    me, lag = device(*coords)
    ahead = 1 - 2 * core

    small_copies = [
        pltpu.make_async_copy(there, here, small_sem.at[index])
        for index, (there, here) in enumerate(((taps_hbm, taps_ref), (lags_hbm, lags_ref), (map_hbm, map_ref)))
    ]
    for copy in small_copies:
        copy.start()
    raw_copies = []
    for index in range(4):
        rows = pl.ds(1280 * index, min(1280, ROWS - 1280 * index))
        raw_copies.append(pltpu.make_async_copy(raw_hbm.at[rows], raw_ref.at[rows], raw_sem.at[index]))
        raw_copies[-1].start()

    def lag_peer(step):
        return me, (lag + step) % 8

    sibling = device(x, y, z, 1 - core)
    barrier = pltpu.get_barrier_semaphore()
    peers = [lag_peer(step) for step in range(1, 8)] + [sibling]
    peers += [device(x, (y + step) % 4, z, core) for step in (1, 3)]
    peers += [device(x, y, (z + step) % 4, core) for step in (1, 3)]
    for peer in peers:
        pl.semaphore_signal(barrier, inc=1, device_id=peer, device_id_type=MESH)

    small_copies[0].wait()
    taps = jnp.broadcast_to(taps_ref[...].astype(F32), (8, TAPS)).astype(BF16)
    spread = lax.broadcasted_iota(jnp.int32, (TAPS, 256), 0) + lax.broadcasted_iota(jnp.int32, (TAPS, 256), 1)
    spread = (spread == 128 + DEC - 1).astype(F32).astype(BF16)
    first = jnp.dot(taps, spread, preferred_element_type=F32)
    first = jnp.concatenate([first, jnp.zeros((8, 512), F32)], axis=1)
    wide = lax.broadcasted_iota(jnp.int32, (8, 768), 0)
    band = first
    for step in range(1, 8):
        band = jnp.where(wide == step, pltpu.roll(first, DEC * step, 1), band)
    band = jnp.concatenate([band] + [pltpu.roll(band, 8 * DEC * step, 1) for step in range(1, 4)], axis=0)
    next_band = pltpu.roll(band[0:16, 0:256], 8, 1).astype(BF16)
    band = band.astype(BF16)

    def tail():
        last = raw_ref[4992:5000].astype(F32)
        last = jnp.concatenate([last, jnp.zeros((8, CB), F32)], axis=0).astype(BF16)
        return [last, jnp.zeros((112, CB), BF16)]

    for part in range(8):
        begin = 640 * part - 128
        if part % 2 == 0:
            raw_copies[part // 2].wait()
        if part == 0:
            piece = jnp.dot(band[:, 128:], raw_ref[0:640], preferred_element_type=F32)
        elif part == 7:
            window = jnp.concatenate([raw_ref[begin:4992]] + tail(), axis=0)
            piece = jnp.dot(band, window, preferred_element_type=F32)
        else:
            piece = jnp.dot(band, raw_ref[begin : begin + 768], preferred_element_type=F32)
        dec_ref[32 * part : 32 * part + 32] = piece
    window = jnp.concatenate([raw_ref[4864:4992]] + tail(), axis=0)
    over = jnp.dot(next_band, window, preferred_element_type=F32)[0:8]

    dec = dec_ref[...]
    sample = lax.broadcasted_iota(jnp.int32, (CB, CB), 0)
    whole = (sample >= HEAD) & (sample < STEP)
    count = STEP - HEAD
    mean = jnp.sum(jnp.where(whole, dec, 0.0), axis=0, keepdims=True) * (1.0 / count)
    spread2 = jnp.where(whole, dec - mean, 0.0)
    energy = jnp.sum(spread2 * spread2, axis=0, keepdims=True)
    line = lax.broadcasted_iota(jnp.int32, (8, CB), 0)
    stat_ref[lag] = jnp.where(
        line == 0,
        mean,
        jnp.where(
            line == 1,
            energy,
            jnp.where(line < 5, pltpu.roll(dec[0:8], 2, 0), pltpu.roll(over, 5, 0)),
        ),
    )
    pl.semaphore_wait(barrier, len(peers))

    def stat_copy(step):
        return pltpu.make_async_remote_copy(
            src_ref=stat_ref.at[lag],
            dst_ref=stat_ref.at[lag],
            send_sem=stat_send.at[step],
            recv_sem=stat_recv.at[step],
            device_id=lag_peer(step),
            device_id_type=MESH,
        )

    for step in range(1, 8):
        stat_copy(step).start()
    row = lax.broadcasted_iota(jnp.int32, (512, 256), 0)
    far = 10000
    time = jnp.where(
        row < 256,
        jnp.where(row < STEP, row, far),
        jnp.where(row < 384, jnp.where(row - 128 < STEP, row - 128 - STEP, far), row - 384 + STEP),
    )
    column = lax.broadcasted_iota(jnp.int32, (512, 256), 1)
    column = jnp.where(column < STEP, column, -far)
    time = time - column
    small_copies[1].wait()
    for slot in range(SLOTS):
        shift_ref[:, CB * slot : CB * slot + CB] = (time == -lags_ref[0:1, slot : slot + 1]).astype(F32).astype(BF16)

    order = lax.broadcasted_iota(jnp.int32, (CB, CB), 0)
    small_copies[2].wait()
    place = (map_ref[...] - (me * CB) == order).astype(F32).astype(BF16)
    for step in range(1, 8):
        stat_copy(step).wait_recv()

    stats = [stat_ref[d] for d in range(8)]
    total = jnp.zeros((8, CB), F32)
    heads = []
    before = jnp.zeros((8, CB), F32)
    for d in range(8):
        head = pltpu.roll(stats[d], 6, 0)
        if d:
            from_left = pltpu.roll(stats[d - 1], 3, 0)
            head = head + from_left
            before = before + jnp.where(lag == d, from_left, 0.0)
        heads.append(head)
        total = total + jnp.where(line < HEAD, head, 0.0)
    mean = count * sum(s[0:1] for s in stats) + jnp.sum(total, axis=0, keepdims=True)
    mean = mean * (1.0 / SAMPLES)
    energy = jnp.zeros((1, CB), F32)
    total = jnp.zeros((8, CB), F32)
    for d in range(8):
        away = stats[d][0:1] - mean
        energy = energy + stats[d][1:2] + count * (away * away)
        away = jnp.where(line < HEAD, heads[d] - mean, 0.0)
        total = total + away * away
    energy = (energy + jnp.sum(total, axis=0, keepdims=True)) * (1.0 / SAMPLES)
    scale = lax.rsqrt(energy + 1e-05)
    dec_ref[0:8] = dec_ref[0:8] + jnp.where(line < HEAD, before, 0.0)
    white = jnp.where(sample < STEP, (dec_ref[...] - mean) * scale, 0.0).astype(BF16)
    ordered = lax.dot_general(white, place, (((1,), (1,)), ((), ())), preferred_element_type=F32)

    there = (0, 1, 2, -1)
    at_x = [(x + 4 + ahead * k) % 4 for k in there]
    at_y = [(y + 4 + ahead * k) % 4 for k in there]
    at_z = [(z + 4 + ahead * k) % 4 for k in there]
    term_y = [(k % 2) * 64 + (k // 2) * 4 for k in at_y]
    term_z = [k * 16 + core * 8 for k in at_z]

    def place_of(offset):
        return at_x[offset[0]] + term_y[offset[1]] + term_z[offset[2]]

    neighbours = {}
    for step in (1, 3):
        neighbours[0, step] = device(at_x[step], y, z, core)
        neighbours[1, step] = device(x, at_y[step], z, core)
        neighbours[2, step] = device(x, y, at_z[step], core)

    g_ref[place_of((0, 0, 0))] = ordered.astype(BF16)

    def block_copy(index):
        offset, axis, row, rows = COPIES[index]
        sent = list(offset)
        sent[axis] = {1: 0, 3: 0, 2: 3}[offset[axis]]
        to = 3 if offset[axis] == 1 else 1
        here = g_ref.at[place_of(sent), pl.ds(row, rows)]
        return pltpu.make_async_remote_copy(
            src_ref=here, dst_ref=here, send_sem=send_sem, recv_sem=recv_sem.at[index],
            device_id=neighbours[axis, to], device_id_type=MESH,
        )

    def block_wait(index):
        offset, axis, row, rows = COPIES[index]
        here = g_ref.at[place_of(offset), pl.ds(row, rows)]
        pltpu.make_async_copy(here, here, recv_sem.at[index]).wait()

    def hand_over(offset):
        here = g_ref.at[place_of(offset)]
        group = (at_y[offset[1]] % 2) * 4 + at_z[offset[2]]
        pltpu.make_async_remote_copy(
            src_ref=here, dst_ref=here, send_sem=other_send, recv_sem=other_recv.at[group],
            device_id=sibling, device_id_type=MESH,
        ).start()

    def taken_over(group):
        channels = group_channels(coords, group, True)
        here = g_ref.at[pl.ds(channels * 8, 8)]
        pltpu.make_async_copy(here, here, other_recv.at[channels // 2]).wait()

    def build_own():
        eye = lax.broadcasted_iota(jnp.int32, (CB, CB), 0) == lax.broadcasted_iota(jnp.int32, (CB, CB), 1)
        eye = eye.astype(F32).astype(BF16)
        turned_ref[0] = jnp.zeros((CB, CB), BF16)
        turned_ref[9] = jnp.zeros((CB, CB), BF16)

        def turn(d, carry):
            turned = lax.dot_general(eye, g_ref[me * 8 + d], (((1,), (1,)), ((), ())), preferred_element_type=F32)
            turned_ref[d + 1] = turned.astype(BF16)
            return carry

        lax.fori_loop(0, 8, turn, 0)

        def shift(d, carry):
            around = jnp.concatenate(
                [turned_ref[d + 1], turned_ref[d, :, 128:256], turned_ref[d + 2, :, 0:128]], axis=1
            )
            moved = jnp.dot(around, shift_ref[...], preferred_element_type=F32)
            for slot in range(SLOTS):
                for half in range(2):
                    begin = CB * slot + 128 * half
                    mixed_ref[half, pl.ds(slot, CB, stride=SLOTS), :] = moved[:, begin : begin + 128]
            for half in range(2):
                there = pl.ds(pl.multiple_of(d * CB + 128 * half, 128), 128)
                lhs_ref[:, there] = mixed_ref[half].astype(BF16)
            return carry

        lax.fori_loop(0, 8, shift, 0)

    def act(actions):
        for kind, what in actions:
            if kind == "w":
                block_wait(what)
            elif kind == "s":
                block_copy(what).start()
            elif kind == "y":
                hand_over(what)
            elif kind == "L":
                build_own()
            elif kind == "D":
                taken_over(what)

    spans, span = [], []
    for action in ACTIONS:
        span.append(action)
        if action[0] in ("C", "D"):
            spans.append(span)
            span = []

    act(spans[0])

    def product(index, carry):
        for number in range(1, len(spans)):
            pl.when(index == number)(functools.partial(act, spans[number]))
        group, other = pick(PRODUCTS, index)
        part_ref[2 * group + other] = multiply(lhs_ref, g_ref, group_channels(coords, group, other))
        return carry

    lax.fori_loop(0, EARLY, product, 0)
    act(span)
    for group in range(EARLY // 2, 8):
        taken_over(group)

    for step in range(1, 8):
        stat_copy(step).wait_send()
    gone = g_ref.at[pl.ds(0, 63)]
    pltpu.make_async_copy(gone, gone, send_sem).wait()
    gone = g_ref.at[pl.ds(0, 64)]
    pltpu.make_async_copy(gone, gone, other_send).wait()


def finish_kernel(part_ref, lhs_ref, g_ref, out_ref, stage_ref, part_sem, stage_sem):
    coords = dims()

    def columns(group, other):
        channels = group_channels(coords, group, other)
        return out_ref.at[:, :, pl.ds(pl.multiple_of(channels * CB, CB), CB)]

    def early_copy(index):
        return pltpu.make_async_copy(part_ref.at[index], columns(index // 2, index % 2), part_sem.at[index])

    def late_copy(index):
        return pltpu.make_async_copy(stage_ref.at[index], columns(*pick(LATE, index)), stage_sem.at[index])

    def early(index, carry):
        early_copy(index).start()
        return carry

    def late(index, carry):
        stage_ref[index] = multiply(lhs_ref, g_ref, group_channels(coords, *pick(LATE, index)))
        late_copy(index).start()
        return carry

    def early_end(index, carry):
        early_copy(index).wait()
        return carry

    def late_end(index, carry):
        late_copy(index).wait()
        return carry

    lax.fori_loop(0, EARLY, early, 0)
    lax.fori_loop(0, len(LATE), late, 0)
    lax.fori_loop(0, EARLY, early_end, 0)
    lax.fori_loop(0, len(LATE), late_end, 0)


def local(raw, fir_taps, channel_map, lag_offsets):
    vmem = pl.BlockSpec(memory_space=pltpu.VMEM)
    given = (raw.T, fir_taps.reshape(1, TAPS), channel_map.reshape(1, CB), lag_offsets.reshape(1, SLOTS))
    hbm = pl.BlockSpec(memory_space=pltpu.HBM)
    part, lhs, blocks = pl.pallas_call(
        gather_kernel,
        out_shape=[
            pltpu.VMEM((EARLY, CB, SLOTS, CB), F32),
            pltpu.VMEM((CB * SLOTS, 8 * CB), BF16),
            pltpu.VMEM((128, CB, CB), BF16),
        ],
        in_specs=[hbm] * 4,
        out_specs=[vmem] * 3,
        scratch_shapes=[
            pltpu.VMEM((ROWS, CB), BF16),
            pltpu.VMEM((1, TAPS), BF16),
            pltpu.VMEM((1, CB), jnp.int32),
            pltpu.VMEM((1, SLOTS), jnp.int32),
            pltpu.VMEM((CB, CB), F32),
            pltpu.VMEM((8, 8, CB), F32),
            pltpu.VMEM((10, CB, CB), BF16),
            pltpu.VMEM((512, SLOTS * CB), BF16),
            pltpu.VMEM((2, CB * SLOTS, 128), F32),
            pltpu.SemaphoreType.DMA((4,)),
            pltpu.SemaphoreType.DMA((3,)),
            pltpu.SemaphoreType.DMA((8,)),
            pltpu.SemaphoreType.DMA((8,)),
            pltpu.SemaphoreType.DMA,
            pltpu.SemaphoreType.DMA((len(COPIES),)),
            pltpu.SemaphoreType.DMA,
            pltpu.SemaphoreType.DMA((8,)),
        ],
        compiler_params=pltpu.CompilerParams(collective_id=0, has_side_effects=True, vmem_limit_bytes=14 << 20),
        name="gather",
    )(*[pltpu.with_memory_space_constraint(a, pltpu.HBM) for a in given])
    part, lhs, blocks = [pltpu.with_memory_space_constraint(a, pltpu.VMEM) for a in (part, lhs, blocks)]
    return pl.pallas_call(
        finish_kernel,
        out_shape=jax.ShapeDtypeStruct((CB, SLOTS, CHANNELS), F32),
        in_specs=[vmem] * 3,
        out_specs=pl.BlockSpec(memory_space=pltpu.HBM),
        scratch_shapes=[
            pltpu.VMEM((len(LATE), CB, SLOTS, CB), F32),
            pltpu.SemaphoreType.DMA((EARLY,)),
            pltpu.SemaphoreType.DMA((len(LATE),)),
        ],
        compiler_params=pltpu.CompilerParams(vmem_limit_bytes=(len(LATE) + 3) << 20),
        name="finish",
    )(part, lhs, blocks)


def solution(mesh):
    placed = (P("chan", "lag"), P(), P("chan"), P("lag"))
    return jax.shard_map(
        local, mesh=mesh, in_specs=placed, out_specs=P("chan", "lag", None), check_vma=False
    )
```

```python
import functools
import math

import jax
import jax.numpy as jnp
from jax import lax
from jax.experimental import pallas as pl
from jax.experimental.pallas import tpu as pltpu
from jax.sharding import PartitionSpec as P

MESH = pl.DeviceIdType.MESH
DEC = 20
TAPS = 80
MAXLAG = 40
CB = 256
SAMPLES = 2000
CHANNELS = 4096
SLOTS = 4
STEP = 250
HEAD = 3
ROWS = 5000
F32, BF16 = jnp.float32, jnp.bfloat16

COPIES = (
    ((0, 0, 1), 2, 0, 80), ((0, 0, 1), 2, 80, 80), ((0, 0, 1), 2, 160, 96), ((0, 0, 2), 2, 0, 256),
    ((0, 0, 3), 2, 0, 80), ((0, 0, 3), 2, 80, 80), ((0, 0, 3), 2, 160, 96), ((0, 1, 0), 1, 0, 80),
    ((0, 1, 0), 1, 80, 80), ((0, 1, 0), 1, 160, 96), ((0, 1, 1), 1, 0, 80), ((0, 1, 1), 2, 80, 176),
    ((0, 1, 2), 1, 0, 256), ((0, 1, 3), 2, 0, 256), ((0, 2, 0), 1, 0, 256), ((0, 2, 1), 2, 0, 256),
    ((0, 2, 2), 1, 0, 256), ((0, 2, 3), 2, 0, 256), ((0, 3, 0), 1, 0, 80), ((0, 3, 0), 1, 80, 80),
    ((0, 3, 0), 1, 160, 96), ((0, 3, 1), 2, 0, 256), ((0, 3, 2), 2, 0, 256), ((0, 3, 3), 2, 0, 256),
    ((1, 0, 0), 0, 0, 80), ((1, 0, 0), 0, 80, 80), ((1, 0, 0), 0, 160, 96), ((1, 0, 1), 2, 0, 256),
    ((1, 0, 2), 0, 0, 256), ((1, 0, 3), 0, 0, 160), ((1, 0, 3), 2, 160, 96), ((1, 1, 0), 1, 0, 256),
    ((1, 1, 1), 1, 0, 256), ((1, 1, 2), 0, 0, 256), ((1, 1, 3), 0, 0, 256), ((1, 2, 0), 1, 0, 256),
    ((1, 2, 1), 1, 0, 256), ((1, 2, 2), 2, 0, 80), ((1, 2, 2), 1, 80, 176), ((1, 2, 3), 2, 0, 256),
    ((1, 3, 0), 1, 0, 256), ((1, 3, 1), 2, 0, 256), ((1, 3, 2), 1, 0, 256), ((1, 3, 3), 1, 0, 256),
    ((2, 0, 0), 0, 0, 256), ((2, 0, 1), 2, 0, 256), ((2, 0, 2), 2, 0, 256), ((2, 0, 3), 0, 0, 256),
    ((2, 1, 0), 1, 0, 160), ((2, 1, 0), 0, 160, 96), ((2, 1, 1), 0, 0, 256), ((2, 1, 2), 0, 0, 256),
    ((2, 1, 3), 2, 0, 256), ((2, 2, 0), 1, 0, 160), ((2, 2, 0), 0, 160, 96), ((2, 2, 1), 2, 0, 256),
    ((2, 2, 2), 2, 0, 256), ((2, 2, 3), 1, 0, 256), ((2, 3, 0), 0, 0, 80), ((2, 3, 0), 0, 160, 96),
    ((2, 3, 0), 1, 80, 80), ((2, 3, 1), 2, 0, 256), ((2, 3, 2), 2, 0, 256), ((2, 3, 3), 1, 0, 256),
    ((3, 0, 0), 0, 0, 80), ((3, 0, 0), 0, 80, 80), ((3, 0, 0), 0, 160, 96), ((3, 0, 1), 0, 0, 80),
    ((3, 0, 1), 0, 160, 96), ((3, 0, 1), 2, 80, 80), ((3, 0, 2), 0, 0, 256), ((3, 0, 3), 0, 0, 80),
    ((3, 0, 3), 0, 160, 96), ((3, 0, 3), 2, 80, 80), ((3, 1, 0), 0, 0, 256), ((3, 1, 1), 2, 0, 256),
    ((3, 1, 2), 0, 0, 256), ((3, 1, 3), 0, 0, 256), ((3, 2, 0), 0, 0, 80), ((3, 2, 0), 0, 160, 96),
    ((3, 2, 0), 1, 80, 80), ((3, 2, 1), 1, 0, 80), ((3, 2, 1), 0, 80, 176), ((3, 2, 2), 2, 0, 256),
    ((3, 2, 3), 2, 0, 256), ((3, 3, 0), 0, 0, 80), ((3, 3, 0), 0, 160, 96), ((3, 3, 0), 1, 80, 80),
    ((3, 3, 1), 1, 0, 80), ((3, 3, 1), 2, 80, 176), ((3, 3, 2), 1, 0, 256), ((3, 3, 3), 1, 0, 80),
    ((3, 3, 3), 2, 80, 80), ((3, 3, 3), 0, 160, 96),
)
ACTIONS = (
    ("s", 64), ("s", 18), ("s", 0), ("s", 65), ("s", 19), ("s", 4), ("s", 66), ("s", 20), ("s", 6), ("s", 24),
    ("s", 7), ("s", 2), ("s", 25), ("s", 8), ("s", 1), ("s", 26), ("s", 9), ("s", 5), ("y", (0, 0, 0)), ("w", 18),
    ("s", 85), ("w", 0), ("s", 10), ("s", 67), ("w", 65), ("s", 87), ("s", 73), ("w", 4), ("s", 71), ("s", 69),
    ("w", 64), ("w", 66), ("s", 44), ("w", 19), ("w", 20), ("s", 14), ("s", 21), ("s", 86), ("s", 23), ("w", 6),
    ("s", 72), ("y", (0, 3, 0)), ("y", (3, 0, 0)), ("w", 2), ("s", 68), ("w", 1), ("y", (0, 0, 1)), ("w", 24),
    ("w", 25), ("w", 26), ("s", 40), ("s", 27), ("w", 8), ("w", 9), ("w", 7), ("s", 74), ("s", 31), ("s", 11),
    ("w", 5), ("s", 29), ("s", 3), ("s", 30), ("s", 13), ("y", (0, 0, 3)), ("y", (0, 1, 0)), ("y", (1, 0, 0)),
    ("w", 85), ("s", 58), ("w", 67), ("s", 88), ("w", 87), ("s", 92), ("s", 80), ("w", 71), ("s", 91), ("w", 14),
    ("s", 79), ("s", 15), ("s", 78), ("w", 44), ("s", 60), ("s", 45), ("s", 48), ("s", 17), ("y", (0, 2, 0)),
    ("w", 21), ("y", (0, 3, 1)), ("y", (2, 0, 0)), ("w", 86), ("y", (3, 3, 0)), ("s", 59), ("s", 89), ("w", 72),
    ("w", 73), ("s", 47), ("w", 40), ("s", 35), ("s", 41), ("y", (1, 3, 0)), ("y", (3, 0, 3)), ("w", 23), ("s", 93),
    ("s", 22), ("y", (0, 3, 3)), ("w", 68), ("w", 69), ("y", (3, 0, 1)), ("w", 31), ("y", (1, 1, 0)), ("w", 27),
    ("s", 32), ("y", (1, 0, 1)), ("w", 74), ("s", 49), ("w", 88), ("s", 81), ("s", 75), ("y", (3, 1, 0)), ("w", 10),
    ("w", 11), ("y", (0, 1, 1)), ("w", 58), ("w", 60), ("s", 53), ("w", 79), ("s", 54), ("w", 3), ("s", 28),
    ("s", 12), ("w", 80), ("w", 78), ("s", 84), ("s", 70), ("y", (0, 0, 2)), ("y", (3, 2, 0)), ("w", 29), ("w", 30),
    ("s", 43), ("w", 59), ("s", 61), ("y", (1, 0, 3)), ("y", (2, 3, 0)), ("w", 35), ("s", 39), ("y", (1, 2, 0)),
    ("w", 13), ("s", 34), ("w", 47), ("s", 63), ("s", 46), ("s", 77), ("y", (0, 1, 3)), ("y", (2, 0, 3)), ("w", 91),
    ("w", 92), ("w", 93), ("y", (3, 3, 3)), ("w", 32), ("y", (1, 1, 1)), ("w", 48), ("w", 49), ("s", 52),
    ("y", (2, 1, 0)), ("w", 15), ("s", 82), ("y", (0, 2, 1)), ("w", 53), ("w", 54), ("s", 55), ("y", (2, 2, 0)),
    ("L", 0), ("w", 12), ("s", 76), ("w", 41), ("s", 36), ("w", 63), ("s", 62), ("s", 33), ("s", 57), ("w", 28),
    ("s", 42), ("w", 70), ("s", 90), ("y", (0, 1, 2)), ("w", 17), ("y", (0, 2, 3)), ("y", (1, 0, 2)), ("w", 34),
    ("y", (1, 1, 3)), ("y", (1, 3, 1)), ("w", 43), ("y", (1, 3, 3)), ("w", 45), ("y", (2, 0, 1)), ("y", (2, 3, 3)),
    ("y", (3, 0, 2)), ("w", 77), ("y", (3, 1, 3)), ("w", 81), ("w", 82), ("y", (3, 2, 1)), ("w", 89),
    ("y", (3, 3, 1)), ("w", 22), ("s", 16), ("y", (0, 3, 2)), ("C", 1), ("w", 75), ("s", 50), ("y", (3, 1, 1)),
    ("C", 0), ("w", 84), ("s", 83), ("y", (3, 2, 3)), ("D", 1), ("w", 76), ("s", 51), ("w", 36), ("y", (1, 2, 1)),
    ("w", 61), ("y", (2, 3, 1)), ("y", (3, 1, 2)), ("w", 39), ("s", 37), ("w", 57), ("s", 56), ("w", 33),
    ("y", (1, 1, 2)), ("y", (1, 2, 3)), ("y", (2, 2, 3)), ("D", 0), ("w", 42), ("s", 38), ("y", (1, 3, 2)),
    ("w", 46), ("y", (2, 0, 2)), ("w", 50), ("y", (2, 1, 1)), ("C", 4), ("w", 52), ("y", (2, 1, 3)), ("w", 90),
    ("y", (3, 3, 2)), ("D", 4), ("w", 16), ("y", (0, 2, 2)), ("w", 51), ("y", (2, 1, 2)), ("w", 55),
    ("y", (2, 2, 1)), ("C", 3), ("w", 62), ("y", (2, 3, 2)), ("D", 3), ("w", 37), ("w", 38), ("y", (1, 2, 2)),
    ("w", 83), ("y", (3, 2, 2)), ("C", 5), ("w", 56), ("y", (2, 2, 2)), ("D", 5), ("C", 2),
)

PRODUCTS = [(what, int(kind == "D")) for kind, what in ACTIONS if kind in ("C", "D")]
LATE = [(group, other) for group in range(8) for other in range(2) if (group, other) not in PRODUCTS]
EARLY = len(PRODUCTS)


def digits(values, bits):
    return sum(value << (bits * index) for index, value in enumerate(values))


def digit(packed, index, bits):
    return lax.shift_right_logical(jnp.int32(packed), index * bits) & ((1 << bits) - 1)


def pick(products, index):
    group = digit(digits([g % 2 for g, _ in products], 1), index, 1)
    group += 2 * digit(digits([g // 2 for g, _ in products], 2), index, 2)
    return group, digit(digits([o for _, o in products], 1), index, 1)


def dims():
    chan, lag = lax.axis_index("chan"), lax.axis_index("lag")
    core, z, y_lo = chan % 2, (chan // 2) % 4, chan // 8
    x, y = lag % 4, (lag // 4) * 2 + y_lo
    return x, y, z, core


def device(x, y, z, core):
    return (((y % 2) * 4 + z) * 2 + core, (y // 2) * 4 + x)


def group_channels(coords, group, other):
    _, y, z, core = coords
    sign = (1 - 2 * core) * (1 - 2 * other)
    step = group // 2
    step = step + (step // 2) * (5 - 2 * step)
    z_there = (z + 4 + sign * (step - 4 * (step // 3))) % 4
    core_there = core + other - 2 * core * other
    return (((y + group) % 2) * 4 + z_there) * 2 + core_there


def multiply(lhs_ref, g_ref, channels):
    block = g_ref[pl.ds(channels * 8, 8)].reshape(8 * CB, CB)
    product = jnp.dot(lhs_ref[...], block, preferred_element_type=F32)
    return (product * (1.0 / math.sqrt(SAMPLES))).reshape(CB, SLOTS, CB)


def gather_kernel(
    raw_hbm, taps_hbm, map_hbm, lags_hbm, part_ref, lhs_ref, g_ref,
    raw_ref, taps_ref, map_ref, lags_ref, dec_ref, stat_ref, turned_ref, shift_ref, mixed_ref,
    raw_sem, small_sem, stat_send, stat_recv, send_sem, recv_sem, other_send, other_recv,
):
    coords = x, y, z, core = dims()
    me, lag = device(*coords)
    ahead = 1 - 2 * core

    small_copies = [
        pltpu.make_async_copy(there, here, small_sem.at[index])
        for index, (there, here) in enumerate(((taps_hbm, taps_ref), (lags_hbm, lags_ref), (map_hbm, map_ref)))
    ]
    for copy in small_copies:
        copy.start()
    raw_copies = []
    for index in range(4):
        rows = pl.ds(1280 * index, min(1280, ROWS - 1280 * index))
        raw_copies.append(pltpu.make_async_copy(raw_hbm.at[rows], raw_ref.at[rows], raw_sem.at[index]))
        raw_copies[-1].start()

    def lag_peer(step):
        return me, (lag + step) % 8

    sibling = device(x, y, z, 1 - core)
    barrier = pltpu.get_barrier_semaphore()
    peers = [lag_peer(step) for step in range(1, 8)] + [sibling]
    peers += [device(x, (y + step) % 4, z, core) for step in (1, 3)]
    peers += [device(x, y, (z + step) % 4, core) for step in (1, 2, 3)]
    for peer in peers:
        pl.semaphore_signal(barrier, inc=1, device_id=peer, device_id_type=MESH)

    small_copies[0].wait()
    taps = jnp.broadcast_to(taps_ref[...].astype(F32), (8, TAPS)).astype(BF16)
    spread = lax.broadcasted_iota(jnp.int32, (TAPS, 256), 0) + lax.broadcasted_iota(jnp.int32, (TAPS, 256), 1)
    spread = (spread == 128 + DEC - 1).astype(F32).astype(BF16)
    first = jnp.dot(taps, spread, preferred_element_type=F32)
    first = jnp.concatenate([first, jnp.zeros((8, 512), F32)], axis=1)
    wide = lax.broadcasted_iota(jnp.int32, (8, 768), 0)
    band = first
    for step in range(1, 8):
        band = jnp.where(wide == step, pltpu.roll(first, DEC * step, 1), band)
    band = jnp.concatenate([band] + [pltpu.roll(band, 8 * DEC * step, 1) for step in range(1, 4)], axis=0)
    next_band = pltpu.roll(band[0:16, 0:256], 8, 1).astype(BF16)
    band = band.astype(BF16)

    def tail():
        last = raw_ref[4992:5000].astype(F32)
        last = jnp.concatenate([last, jnp.zeros((8, CB), F32)], axis=0).astype(BF16)
        return [last, jnp.zeros((112, CB), BF16)]

    for part in range(8):
        begin = 640 * part - 128
        if part % 2 == 0:
            raw_copies[part // 2].wait()
        if part == 0:
            piece = jnp.dot(band[:, 128:], raw_ref[0:640], preferred_element_type=F32)
        elif part == 7:
            window = jnp.concatenate([raw_ref[begin:4992]] + tail(), axis=0)
            piece = jnp.dot(band, window, preferred_element_type=F32)
        else:
            piece = jnp.dot(band, raw_ref[begin : begin + 768], preferred_element_type=F32)
        dec_ref[32 * part : 32 * part + 32] = piece
    window = jnp.concatenate([raw_ref[4864:4992]] + tail(), axis=0)
    over = jnp.dot(next_band, window, preferred_element_type=F32)[0:8]

    dec = dec_ref[...]
    sample = lax.broadcasted_iota(jnp.int32, (CB, CB), 0)
    whole = (sample >= HEAD) & (sample < STEP)
    count = STEP - HEAD
    mean = jnp.sum(jnp.where(whole, dec, 0.0), axis=0, keepdims=True) * (1.0 / count)
    spread2 = jnp.where(whole, dec - mean, 0.0)
    energy = jnp.sum(spread2 * spread2, axis=0, keepdims=True)
    line = lax.broadcasted_iota(jnp.int32, (8, CB), 0)
    stat_ref[lag] = jnp.where(
        line == 0,
        mean,
        jnp.where(
            line == 1,
            energy,
            jnp.where(line < 5, pltpu.roll(dec[0:8], 2, 0), pltpu.roll(over, 5, 0)),
        ),
    )
    pl.semaphore_wait(barrier, len(peers))

    def stat_copy(step):
        return pltpu.make_async_remote_copy(
            src_ref=stat_ref.at[lag],
            dst_ref=stat_ref.at[lag],
            send_sem=stat_send.at[step],
            recv_sem=stat_recv.at[step],
            device_id=lag_peer(step),
            device_id_type=MESH,
        )

    for step in range(1, 8):
        stat_copy(step).start()
    row = lax.broadcasted_iota(jnp.int32, (512, 256), 0)
    far = 10000
    time = jnp.where(
        row < 256,
        jnp.where(row < STEP, row, far),
        jnp.where(row < 384, jnp.where(row - 128 < STEP, row - 128 - STEP, far), row - 384 + STEP),
    )
    column = lax.broadcasted_iota(jnp.int32, (512, 256), 1)
    column = jnp.where(column < STEP, column, -far)
    time = time - column
    small_copies[1].wait()
    for slot in range(SLOTS):
        shift_ref[:, CB * slot : CB * slot + CB] = (time == -lags_ref[0:1, slot : slot + 1]).astype(F32).astype(BF16)

    order = lax.broadcasted_iota(jnp.int32, (CB, CB), 0)
    small_copies[2].wait()
    place = (map_ref[...] - (me * CB) == order).astype(F32).astype(BF16)
    for step in range(1, 8):
        stat_copy(step).wait_recv()

    stats = [stat_ref[d] for d in range(8)]
    total = jnp.zeros((8, CB), F32)
    heads = []
    before = jnp.zeros((8, CB), F32)
    for d in range(8):
        head = pltpu.roll(stats[d], 6, 0)
        if d:
            from_left = pltpu.roll(stats[d - 1], 3, 0)
            head = head + from_left
            before = before + jnp.where(lag == d, from_left, 0.0)
        heads.append(head)
        total = total + jnp.where(line < HEAD, head, 0.0)
    mean = count * sum(s[0:1] for s in stats) + jnp.sum(total, axis=0, keepdims=True)
    mean = mean * (1.0 / SAMPLES)
    energy = jnp.zeros((1, CB), F32)
    total = jnp.zeros((8, CB), F32)
    for d in range(8):
        away = stats[d][0:1] - mean
        energy = energy + stats[d][1:2] + count * (away * away)
        away = jnp.where(line < HEAD, heads[d] - mean, 0.0)
        total = total + away * away
    energy = (energy + jnp.sum(total, axis=0, keepdims=True)) * (1.0 / SAMPLES)
    scale = lax.rsqrt(energy + 1e-05)
    dec_ref[0:8] = dec_ref[0:8] + jnp.where(line < HEAD, before, 0.0)
    white = jnp.where(sample < STEP, (dec_ref[...] - mean) * scale, 0.0).astype(BF16)
    ordered = lax.dot_general(white, place, (((1,), (1,)), ((), ())), preferred_element_type=F32)

    there = (0, 1, 2, -1)
    at_x = [(x + 4 + ahead * k) % 4 for k in there]
    at_y = [(y + 4 + ahead * k) % 4 for k in there]
    at_z = [(z + 4 + ahead * k) % 4 for k in there]
    term_y = [(k % 2) * 64 + (k // 2) * 4 for k in at_y]
    term_z = [k * 16 + core * 8 for k in at_z]

    def place_of(offset):
        return at_x[offset[0]] + term_y[offset[1]] + term_z[offset[2]]

    neighbours = {}
    for step in (1, 2, 3):
        neighbours[0, step] = device(at_x[step], y, z, core)
        neighbours[1, step] = device(x, at_y[step], z, core)
        neighbours[2, step] = device(x, y, at_z[step], core)

    g_ref[place_of((0, 0, 0))] = ordered.astype(BF16)
    turned_ref[0] = jnp.zeros((CB, CB), BF16)
    turned_ref[9] = jnp.zeros((CB, CB), BF16)

    def block_copy(index):
        offset, axis, row, rows = COPIES[index]
        axis, far = axis % 3, axis // 3
        sent = list(offset)
        sent[axis] = {1: 0, 3: 0, 2: 0 if far else 3}[offset[axis]]
        to = 2 if far else 3 if offset[axis] == 1 else 1
        here = g_ref.at[place_of(sent), pl.ds(row, rows)]
        return pltpu.make_async_remote_copy(
            src_ref=here, dst_ref=here, send_sem=send_sem, recv_sem=recv_sem.at[index],
            device_id=neighbours[axis, to], device_id_type=MESH,
        )

    def block_wait(index):
        offset, axis, row, rows = COPIES[index]
        here = g_ref.at[place_of(offset), pl.ds(row, rows)]
        pltpu.make_async_copy(here, here, recv_sem.at[index]).wait()

    def hand_over(offset):
        here = g_ref.at[place_of(offset)]
        group = (at_y[offset[1]] % 2) * 4 + at_z[offset[2]]
        pltpu.make_async_remote_copy(
            src_ref=here, dst_ref=here, send_sem=other_send, recv_sem=other_recv.at[group],
            device_id=sibling, device_id_type=MESH,
        ).start()

    def taken_over(group):
        channels = group_channels(coords, group, True)
        here = g_ref.at[pl.ds(channels * 8, 8)]
        pltpu.make_async_copy(here, here, other_recv.at[channels // 2]).wait()

    eye = lax.broadcasted_iota(jnp.int32, (CB, CB), 0) == lax.broadcasted_iota(jnp.int32, (CB, CB), 1)
    eye = eye.astype(F32).astype(BF16)

    def turn(offset):
        block = g_ref[place_of(offset)]
        turned = lax.dot_general(eye, block, (((1,), (1,)), ((), ())), preferred_element_type=F32)
        turned_ref[(at_y[offset[1]] // 2) * 4 + at_x[offset[0]] + 1] = turned.astype(BF16)

    def build_own():
        def shift(pair, carry):
            for part in range(2):
                d = pair * 2 + part
                around = jnp.concatenate(
                    [turned_ref[d + 1], turned_ref[d, :, 128:256], turned_ref[d + 2, :, 0:128]], axis=1
                )
                moved = jnp.dot(around, shift_ref[...], preferred_element_type=F32)
                for slot in range(SLOTS):
                    for half in range(2):
                        begin = CB * slot + 128 * half
                        mixed_ref[2 * part + half, pl.ds(slot, CB, stride=SLOTS), :] = moved[:, begin : begin + 128]
                for half in range(2):
                    there = pl.ds(pl.multiple_of(d * CB + 128 * half, 128), 128)
                    lhs_ref[:, there] = mixed_ref[2 * part + half].astype(BF16)
            return carry

        lax.fori_loop(0, 4, shift, 0)

    def act(actions):
        for kind, what in actions:
            if kind == "w":
                block_wait(what)
            elif kind == "s":
                block_copy(what).start()
            elif kind == "y":
                hand_over(what)
                if what[1] in (0, 2) and what[2] == 0:
                    turn(what)
            elif kind == "L":
                build_own()
            elif kind == "D":
                taken_over(what)

    spans, span = [], []
    for action in ACTIONS:
        span.append(action)
        if action[0] in ("C", "D"):
            spans.append(span)
            span = []

    act(spans[0])

    def product(index, carry):
        for number in range(1, len(spans)):
            pl.when(index == number)(functools.partial(act, spans[number]))
        group, other = pick(PRODUCTS, index)
        part_ref[index] = multiply(lhs_ref, g_ref, group_channels(coords, group, other))
        return carry

    lax.fori_loop(0, EARLY, product, 0)
    act(span)
    for group, other in LATE:
        if other:
            taken_over(group)

    for step in range(1, 8):
        stat_copy(step).wait_send()
    gone = g_ref.at[pl.ds(0, 63)]
    pltpu.make_async_copy(gone, gone, send_sem).wait()
    gone = g_ref.at[pl.ds(0, 64)]
    pltpu.make_async_copy(gone, gone, other_send).wait()


def finish_kernel(part_ref, lhs_ref, g_ref, out_ref, stage_ref, part_sem, stage_sem):
    coords = dims()

    def columns(group, other):
        channels = group_channels(coords, group, other)
        return out_ref.at[:, :, pl.ds(pl.multiple_of(channels * CB, CB), CB)]

    def early_copy(index):
        return pltpu.make_async_copy(part_ref.at[index], columns(*pick(PRODUCTS, index)), part_sem.at[index])

    def late_copy(index):
        return pltpu.make_async_copy(stage_ref.at[index], columns(*pick(LATE, index)), stage_sem.at[index])

    def early(index, carry):
        early_copy(index).start()
        return carry

    def late(index, carry):
        stage_ref[index] = multiply(lhs_ref, g_ref, group_channels(coords, *pick(LATE, index)))
        late_copy(index).start()
        return carry

    def early_end(index, carry):
        early_copy(index).wait()
        return carry

    def late_end(index, carry):
        late_copy(index).wait()
        return carry

    lax.fori_loop(0, EARLY, early, 0)
    lax.fori_loop(0, len(LATE), late, 0)
    lax.fori_loop(0, EARLY, early_end, 0)
    lax.fori_loop(0, len(LATE), late_end, 0)


def local(raw, fir_taps, channel_map, lag_offsets):
    vmem = pl.BlockSpec(memory_space=pltpu.VMEM)
    given = (raw.T, fir_taps.reshape(1, TAPS), channel_map.reshape(1, CB), lag_offsets.reshape(1, SLOTS))
    hbm = pl.BlockSpec(memory_space=pltpu.HBM)
    part, lhs, blocks = pl.pallas_call(
        gather_kernel,
        out_shape=[
            pltpu.VMEM((EARLY, CB, SLOTS, CB), F32),
            pltpu.VMEM((CB * SLOTS, 8 * CB), BF16),
            pltpu.VMEM((128, CB, CB), BF16),
        ],
        in_specs=[hbm] * 4,
        out_specs=[vmem] * 3,
        scratch_shapes=[
            pltpu.VMEM((ROWS, CB), BF16),
            pltpu.VMEM((1, TAPS), BF16),
            pltpu.VMEM((1, CB), jnp.int32),
            pltpu.VMEM((1, SLOTS), jnp.int32),
            pltpu.VMEM((CB, CB), F32),
            pltpu.VMEM((8, 8, CB), F32),
            pltpu.VMEM((10, CB, CB), BF16),
            pltpu.VMEM((512, SLOTS * CB), BF16),
            pltpu.VMEM((4, CB * SLOTS, 128), F32),
            pltpu.SemaphoreType.DMA((4,)),
            pltpu.SemaphoreType.DMA((3,)),
            pltpu.SemaphoreType.DMA((8,)),
            pltpu.SemaphoreType.DMA((8,)),
            pltpu.SemaphoreType.DMA,
            pltpu.SemaphoreType.DMA((len(COPIES),)),
            pltpu.SemaphoreType.DMA,
            pltpu.SemaphoreType.DMA((8,)),
        ],
        compiler_params=pltpu.CompilerParams(collective_id=0, has_side_effects=True, vmem_limit_bytes=14 << 20),
        name="gather",
    )(*[pltpu.with_memory_space_constraint(a, pltpu.HBM) for a in given])
    part, lhs, blocks = [pltpu.with_memory_space_constraint(a, pltpu.VMEM) for a in (part, lhs, blocks)]
    return pl.pallas_call(
        finish_kernel,
        out_shape=jax.ShapeDtypeStruct((CB, SLOTS, CHANNELS), F32),
        in_specs=[vmem] * 3,
        out_specs=pl.BlockSpec(memory_space=pltpu.HBM),
        scratch_shapes=[
            pltpu.VMEM((len(LATE), CB, SLOTS, CB), F32),
            pltpu.SemaphoreType.DMA((EARLY,)),
            pltpu.SemaphoreType.DMA((len(LATE),)),
        ],
        compiler_params=pltpu.CompilerParams(vmem_limit_bytes=(len(LATE) + 3) << 20),
        name="finish",
    )(part, lhs, blocks)


def solution(mesh):
    placed = (P("chan", "lag"), P(), P("chan"), P("lag"))
    return jax.shard_map(
        local, mesh=mesh, in_specs=placed, out_specs=P("chan", "lag", None), check_vma=False
    )
```

```python
import functools
import math

import jax
import jax.numpy as jnp
from jax import lax
from jax.experimental import pallas as pl
from jax.experimental.pallas import tpu as pltpu
from jax.sharding import PartitionSpec as P

MESH = pl.DeviceIdType.MESH
DEC = 20
TAPS = 80
MAXLAG = 40
CB = 256
SAMPLES = 2000
CHANNELS = 4096
SLOTS = 4
STEP = 250
HEAD = 3
ROWS = 5000
F32, BF16 = jnp.float32, jnp.bfloat16

COPIES = (
    ((0, 0, 1), 2, 0, 80), ((0, 0, 1), 2, 80, 80), ((0, 0, 1), 2, 160, 96), ((0, 0, 2), 2, 0, 256),
    ((0, 0, 3), 2, 0, 80), ((0, 0, 3), 2, 80, 80), ((0, 0, 3), 2, 160, 96), ((0, 1, 0), 1, 0, 80),
    ((0, 1, 0), 1, 80, 80), ((0, 1, 0), 1, 160, 96), ((0, 1, 1), 2, 0, 256), ((0, 1, 2), 2, 0, 256),
    ((0, 1, 3), 2, 0, 256), ((0, 2, 0), 1, 0, 256), ((0, 2, 1), 1, 0, 256), ((0, 2, 2), 1, 0, 256),
    ((0, 2, 3), 2, 0, 256), ((0, 3, 0), 1, 0, 80), ((0, 3, 0), 1, 80, 80), ((0, 3, 0), 1, 160, 96),
    ((0, 3, 1), 1, 0, 80), ((0, 3, 1), 2, 80, 176), ((0, 3, 2), 1, 0, 256), ((0, 3, 3), 2, 0, 256),
    ((1, 0, 0), 0, 0, 80), ((1, 0, 0), 0, 80, 80), ((1, 0, 0), 0, 160, 96), ((1, 0, 1), 2, 0, 256),
    ((1, 0, 2), 2, 0, 256), ((1, 0, 3), 0, 0, 80), ((1, 0, 3), 2, 80, 176), ((1, 1, 0), 1, 0, 160),
    ((1, 1, 0), 0, 160, 96), ((1, 1, 1), 0, 0, 256), ((1, 1, 2), 0, 0, 256), ((1, 1, 3), 1, 0, 256),
    ((1, 2, 0), 1, 0, 80), ((1, 2, 0), 0, 80, 176), ((1, 2, 1), 0, 0, 256), ((1, 2, 2), 0, 0, 256),
    ((1, 2, 3), 1, 0, 256), ((1, 3, 0), 1, 0, 256), ((1, 3, 1), 1, 0, 80), ((1, 3, 1), 1, 160, 96),
    ((1, 3, 1), 2, 80, 80), ((1, 3, 2), 1, 0, 256), ((1, 3, 3), 1, 0, 256), ((2, 0, 0), 0, 0, 256),
    ((2, 0, 1), 2, 0, 80), ((2, 0, 1), 0, 80, 176), ((2, 0, 2), 2, 0, 256), ((2, 0, 3), 0, 0, 256),
    ((2, 1, 0), 0, 0, 256), ((2, 1, 1), 2, 0, 256), ((2, 1, 2), 2, 0, 256), ((2, 1, 3), 2, 0, 256),
    ((2, 2, 0), 1, 0, 80), ((2, 2, 0), 0, 80, 176), ((2, 2, 1), 1, 0, 256), ((2, 2, 2), 2, 0, 256),
    ((2, 2, 3), 1, 0, 256), ((2, 3, 0), 0, 0, 80), ((2, 3, 0), 1, 80, 176), ((2, 3, 1), 1, 0, 256),
    ((2, 3, 2), 2, 0, 256), ((2, 3, 3), 1, 0, 256), ((3, 0, 0), 0, 0, 80), ((3, 0, 0), 0, 80, 80),
    ((3, 0, 0), 0, 160, 96), ((3, 0, 1), 2, 0, 160), ((3, 0, 1), 0, 160, 96), ((3, 0, 2), 2, 0, 256),
    ((3, 0, 3), 0, 0, 160), ((3, 0, 3), 2, 160, 96), ((3, 1, 0), 1, 0, 256), ((3, 1, 1), 0, 0, 256),
    ((3, 1, 2), 1, 0, 256), ((3, 1, 3), 0, 0, 256), ((3, 2, 0), 1, 0, 160), ((3, 2, 0), 0, 160, 96),
    ((3, 2, 1), 0, 0, 256), ((3, 2, 2), 0, 0, 256), ((3, 2, 3), 2, 0, 256), ((3, 3, 0), 0, 0, 80),
    ((3, 3, 0), 0, 160, 96), ((3, 3, 0), 1, 80, 80), ((3, 3, 1), 2, 0, 256), ((3, 3, 2), 0, 0, 256),
    ((3, 3, 3), 2, 0, 256),
)
ACTIONS = (
    ("s", 67), ("s", 17), ("s", 2), ("s", 66), ("s", 18), ("s", 0), ("s", 68), ("s", 19), ("s", 4), ("s", 24),
    ("s", 9), ("s", 5), ("s", 25), ("s", 7), ("s", 6), ("s", 26), ("s", 8), ("s", 1), ("w", 67), ("s", 85),
    ("w", 17), ("s", 83), ("w", 2), ("s", 70), ("w", 66), ("s", 69), ("w", 0), ("s", 20), ("w", 68), ("s", 47),
    ("w", 18), ("w", 19), ("s", 13), ("s", 21), ("s", 84), ("s", 74), ("s", 73), ("w", 4), ("s", 29), ("s", 23),
    ("w", 5), ("s", 72), ("w", 9), ("s", 32), ("w", 24), ("w", 25), ("s", 31), ("w", 6), ("s", 3), ("w", 26),
    ("s", 41), ("s", 30), ("w", 8), ("w", 7), ("s", 10), ("s", 27), ("s", 12), ("w", 83), ("s", 61), ("w", 85),
    ("s", 78), ("w", 69), ("w", 70), ("s", 49), ("w", 20), ("w", 21), ("s", 14), ("w", 47), ("s", 62), ("s", 48),
    ("w", 13), ("s", 79), ("s", 16), ("s", 37), ("y", (0, 0)), ("w", 74), ("s", 52), ("w", 84), ("s", 86),
    ("w", 72), ("w", 73), ("s", 51), ("s", 88), ("s", 71), ("w", 61), ("s", 56), ("w", 3), ("s", 22), ("w", 41),
    ("s", 36), ("s", 44), ("w", 29), ("w", 30), ("s", 46), ("s", 28), ("s", 35), ("w", 78), ("w", 79), ("s", 57),
    ("s", 82), ("w", 10), ("s", 33), ("s", 75), ("w", 14), ("s", 38), ("s", 80), ("w", 27), ("s", 42), ("s", 43),
    ("w", 62), ("y", (3, 0)), ("w", 52), ("s", 53), ("s", 55), ("w", 31), ("w", 32), ("y", (1, 0)), ("w", 12),
    ("s", 77), ("s", 11), ("w", 51), ("s", 65), ("s", 50), ("y", (0, 3)), ("w", 48), ("w", 49), ("s", 63),
    ("w", 22), ("s", 87), ("s", 15), ("w", 1), ("y", (0, 1)), ("w", 36), ("w", 37), ("w", 56), ("w", 57),
    ("y", (2, 0)), ("L", 0), ("w", 46), ("s", 40), ("C", 1), ("w", 65), ("s", 60), ("s", 64), ("w", 71), ("s", 76),
    ("w", 23), ("w", 88), ("y", (3, 3)), ("D", 1), ("w", 63), ("s", 58), ("w", 28), ("s", 45), ("w", 42), ("w", 43),
    ("w", 44), ("w", 86), ("y", (3, 1)), ("w", 15), ("s", 39), ("s", 81), ("C", 0), ("D", 0), ("w", 60), ("s", 59),
    ("w", 33), ("w", 53), ("w", 75), ("y", (1, 1)), ("w", 16), ("w", 40), ("w", 82), ("y", (2, 3)), ("w", 35),
    ("w", 55), ("w", 77), ("y", (1, 3)), ("s", 54), ("C", 3), ("w", 11), ("s", 34), ("C", 4), ("w", 38), ("w", 58),
    ("w", 80), ("y", (2, 1)), ("w", 50), ("y", (0, 2)), ("C", 5), ("w", 45), ("w", 64), ("w", 87), ("y", (3, 2)),
    ("D", 3), ("w", 39), ("w", 59), ("w", 81), ("y", (2, 2)), ("D", 4), ("w", 34), ("w", 54), ("w", 76),
    ("y", (1, 2)), ("D", 5), ("C", 2),
)

PRODUCTS = [(what, int(kind == "D")) for kind, what in ACTIONS if kind in ("C", "D")]
LATE = [(group, other) for group in range(8) for other in range(2) if (group, other) not in PRODUCTS]
EARLY = len(PRODUCTS)


def digits(values, bits):
    return sum(value << (bits * index) for index, value in enumerate(values))


def digit(packed, index, bits):
    return lax.shift_right_logical(jnp.int32(packed), index * bits) & ((1 << bits) - 1)


def pick(products, index):
    group = digit(digits([g % 2 for g, _ in products], 1), index, 1)
    group += 2 * digit(digits([g // 2 for g, _ in products], 2), index, 2)
    return group, digit(digits([o for _, o in products], 1), index, 1)


def dims():
    chan, lag = lax.axis_index("chan"), lax.axis_index("lag")
    core, z, y_lo = chan % 2, (chan // 2) % 4, chan // 8
    x, y = lag % 4, (lag // 4) * 2 + y_lo
    return x, y, z, core


def device(x, y, z, core):
    return (((y % 2) * 4 + z) * 2 + core, (y // 2) * 4 + x)


def group_channels(coords, group, other):
    _, y, z, core = coords
    sign = (1 - 2 * core) * (1 - 2 * other)
    step = group // 2
    step = step + (step // 2) * (5 - 2 * step)
    z_there = (z + 4 + sign * (step - 4 * (step // 3))) % 4
    core_there = core + other - 2 * core * other
    return (((y + group) % 2) * 4 + z_there) * 2 + core_there


def multiply(lhs_ref, g_ref, channels):
    block = g_ref[pl.ds(channels * 8, 8)].reshape(8 * CB, CB)
    product = jnp.dot(lhs_ref[...], block, preferred_element_type=F32)
    return (product * (1.0 / math.sqrt(SAMPLES))).reshape(CB, SLOTS, CB)


def gather_kernel(
    raw_hbm, taps_hbm, map_hbm, lags_hbm, part_ref, lhs_ref, g_ref,
    raw_ref, taps_ref, map_ref, lags_ref, dec_ref, stat_ref, turned_ref, shift_ref, mixed_ref,
    raw_sem, small_sem, stat_send, stat_recv, send_sem, recv_sem, other_send, other_recv,
):
    coords = x, y, z, core = dims()
    me, lag = device(*coords)
    ahead = 1 - 2 * core

    small_copies = [
        pltpu.make_async_copy(there, here, small_sem.at[index])
        for index, (there, here) in enumerate(((taps_hbm, taps_ref), (lags_hbm, lags_ref), (map_hbm, map_ref)))
    ]
    for copy in small_copies:
        copy.start()
    raw_copies = []
    for index in range(4):
        rows = pl.ds(1280 * index, min(1280, ROWS - 1280 * index))
        raw_copies.append(pltpu.make_async_copy(raw_hbm.at[rows], raw_ref.at[rows], raw_sem.at[index]))
        raw_copies[-1].start()

    def lag_peer(step):
        return me, (lag + step) % 8

    sibling = device(x, y, z, 1 - core)
    barrier = pltpu.get_barrier_semaphore()
    peers = [lag_peer(step) for step in range(1, 8)] + [sibling]
    peers += [device(x, (y + step) % 4, z, core) for step in (1, 3)]
    peers += [device(x, y, (z + step) % 4, core) for step in (1, 2, 3)]
    for peer in peers:
        pl.semaphore_signal(barrier, inc=1, device_id=peer, device_id_type=MESH)

    small_copies[0].wait()
    taps = jnp.broadcast_to(taps_ref[...].astype(F32), (8, TAPS)).astype(BF16)
    spread = lax.broadcasted_iota(jnp.int32, (TAPS, 256), 0) + lax.broadcasted_iota(jnp.int32, (TAPS, 256), 1)
    spread = (spread == 128 + DEC - 1).astype(F32).astype(BF16)
    first = jnp.dot(taps, spread, preferred_element_type=F32)
    first = jnp.concatenate([first, jnp.zeros((8, 512), F32)], axis=1)
    wide = lax.broadcasted_iota(jnp.int32, (8, 768), 0)
    band = first
    for step in range(1, 8):
        band = jnp.where(wide == step, pltpu.roll(first, DEC * step, 1), band)
    band = jnp.concatenate([band] + [pltpu.roll(band, 8 * DEC * step, 1) for step in range(1, 4)], axis=0)
    next_band = pltpu.roll(band[0:16, 0:256], 8, 1).astype(BF16)
    band = band.astype(BF16)

    def tail():
        last = raw_ref[4992:5000].astype(F32)
        last = jnp.concatenate([last, jnp.zeros((8, CB), F32)], axis=0).astype(BF16)
        return [last, jnp.zeros((112, CB), BF16)]

    for part in range(8):
        begin = 640 * part - 128
        if part % 2 == 0:
            raw_copies[part // 2].wait()
        if part == 0:
            piece = jnp.dot(band[:, 128:], raw_ref[0:640], preferred_element_type=F32)
        elif part == 7:
            window = jnp.concatenate([raw_ref[begin:4992]] + tail(), axis=0)
            piece = jnp.dot(band, window, preferred_element_type=F32)
        else:
            piece = jnp.dot(band, raw_ref[begin : begin + 768], preferred_element_type=F32)
        dec_ref[32 * part : 32 * part + 32] = piece
    window = jnp.concatenate([raw_ref[4864:4992]] + tail(), axis=0)
    over = jnp.dot(next_band, window, preferred_element_type=F32)[0:8]

    dec = dec_ref[...]
    sample = lax.broadcasted_iota(jnp.int32, (CB, CB), 0)
    whole = (sample >= HEAD) & (sample < STEP)
    count = STEP - HEAD
    mean = jnp.sum(jnp.where(whole, dec, 0.0), axis=0, keepdims=True) * (1.0 / count)
    spread2 = jnp.where(whole, dec - mean, 0.0)
    energy = jnp.sum(spread2 * spread2, axis=0, keepdims=True)
    line = lax.broadcasted_iota(jnp.int32, (8, CB), 0)
    stat_ref[lag] = jnp.where(
        line == 0,
        mean,
        jnp.where(
            line == 1,
            energy,
            jnp.where(line < 5, pltpu.roll(dec[0:8], 2, 0), pltpu.roll(over, 5, 0)),
        ),
    )
    pl.semaphore_wait(barrier, len(peers))

    def stat_copy(step):
        return pltpu.make_async_remote_copy(
            src_ref=stat_ref.at[lag],
            dst_ref=stat_ref.at[lag],
            send_sem=stat_send.at[step],
            recv_sem=stat_recv.at[step],
            device_id=lag_peer(step),
            device_id_type=MESH,
        )

    for step in range(1, 8):
        stat_copy(step).start()
    row = lax.broadcasted_iota(jnp.int32, (512, 256), 0)
    far = 10000
    time = jnp.where(
        row < 256,
        jnp.where(row < STEP, row, far),
        jnp.where(row < 384, jnp.where(row - 128 < STEP, row - 128 - STEP, far), row - 384 + STEP),
    )
    column = lax.broadcasted_iota(jnp.int32, (512, 256), 1)
    column = jnp.where(column < STEP, column, -far)
    time = time - column
    small_copies[1].wait()
    for slot in range(SLOTS):
        shift_ref[:, CB * slot : CB * slot + CB] = (time == -lags_ref[0:1, slot : slot + 1]).astype(F32).astype(BF16)

    order = lax.broadcasted_iota(jnp.int32, (CB, CB), 0)
    small_copies[2].wait()
    place = (map_ref[...] - (me * CB) == order).astype(F32).astype(BF16)
    for step in range(1, 8):
        stat_copy(step).wait_recv()

    stats = [stat_ref[d] for d in range(8)]
    total = jnp.zeros((8, CB), F32)
    heads = []
    before = jnp.zeros((8, CB), F32)
    for d in range(8):
        head = pltpu.roll(stats[d], 6, 0)
        if d:
            from_left = pltpu.roll(stats[d - 1], 3, 0)
            head = head + from_left
            before = before + jnp.where(lag == d, from_left, 0.0)
        heads.append(head)
        total = total + jnp.where(line < HEAD, head, 0.0)
    mean = count * sum(s[0:1] for s in stats) + jnp.sum(total, axis=0, keepdims=True)
    mean = mean * (1.0 / SAMPLES)
    energy = jnp.zeros((1, CB), F32)
    total = jnp.zeros((8, CB), F32)
    for d in range(8):
        away = stats[d][0:1] - mean
        energy = energy + stats[d][1:2] + count * (away * away)
        away = jnp.where(line < HEAD, heads[d] - mean, 0.0)
        total = total + away * away
    energy = (energy + jnp.sum(total, axis=0, keepdims=True)) * (1.0 / SAMPLES)
    scale = lax.rsqrt(energy + 1e-05)
    dec_ref[0:8] = dec_ref[0:8] + jnp.where(line < HEAD, before, 0.0)
    white = jnp.where(sample < STEP, (dec_ref[...] - mean) * scale, 0.0).astype(BF16)
    ordered = lax.dot_general(white, place, (((1,), (1,)), ((), ())), preferred_element_type=F32)

    there = (0, 1, 2, -1)
    at_x = [(x + 4 + ahead * k) % 4 for k in there]
    at_y = [(y + 4 + ahead * k) % 4 for k in there]
    at_z = [(z + 4 + ahead * k) % 4 for k in there]
    term_y = [(k % 2) * 64 + (k // 2) * 4 for k in at_y]
    term_z = [k * 16 + core * 8 for k in at_z]

    def place_of(offset):
        return at_x[offset[0]] + term_y[offset[1]] + term_z[offset[2]]

    neighbours = {}
    for step in (1, 2, 3):
        neighbours[0, step] = device(at_x[step], y, z, core)
        neighbours[1, step] = device(x, at_y[step], z, core)
        neighbours[2, step] = device(x, y, at_z[step], core)

    g_ref[place_of((0, 0, 0))] = ordered.astype(BF16)
    turned_ref[0] = jnp.zeros((CB, CB), BF16)
    turned_ref[9] = jnp.zeros((CB, CB), BF16)

    def block_copy(index):
        offset, axis, row, rows = COPIES[index]
        axis, far = axis % 3, axis // 3
        sent = list(offset)
        sent[axis] = {1: 0, 3: 0, 2: 0 if far else 3}[offset[axis]]
        to = 2 if far else 3 if offset[axis] == 1 else 1
        here = g_ref.at[place_of(sent), pl.ds(row, rows)]
        return pltpu.make_async_remote_copy(
            src_ref=here, dst_ref=here, send_sem=send_sem, recv_sem=recv_sem.at[index],
            device_id=neighbours[axis, to], device_id_type=MESH,
        )

    def block_wait(index):
        offset, axis, row, rows = COPIES[index]
        here = g_ref.at[place_of(offset), pl.ds(row, rows)]
        pltpu.make_async_copy(here, here, recv_sem.at[index]).wait()

    def line_of(offset):
        return pl.ds(term_y[offset[0]] + term_z[offset[1]], 4)

    def hand_over(offset):
        here = g_ref.at[line_of(offset)]
        half = (at_y[offset[0]] % 2) * 4 + at_z[offset[1]] + 8 * (at_y[offset[0]] // 2)
        pltpu.make_async_remote_copy(
            src_ref=here, dst_ref=here, send_sem=other_send, recv_sem=other_recv.at[half],
            device_id=sibling, device_id_type=MESH,
        ).start()

    def taken_over(group):
        channels = group_channels(coords, group, True)
        for half in range(2):
            here = g_ref.at[pl.ds(channels * 8 + 4 * half, 4)]
            pltpu.make_async_copy(here, here, other_recv.at[channels // 2 + 8 * half]).wait()

    eye = lax.broadcasted_iota(jnp.int32, (CB, CB), 0) == lax.broadcasted_iota(jnp.int32, (CB, CB), 1)
    eye = eye.astype(F32).astype(BF16)

    def turn(offset):
        first = (at_y[offset[0]] // 2) * 4
        for part in range(4):
            block = g_ref[me * 8 + first + part]
            turned = lax.dot_general(eye, block, (((1,), (1,)), ((), ())), preferred_element_type=F32)
            turned_ref[first + part + 1] = turned.astype(BF16)

    def shift(*pair):
        for part, d in enumerate(pair):
            around = jnp.concatenate(
                [turned_ref[d + 1], turned_ref[d, :, 128:256], turned_ref[d + 2, :, 0:128]], axis=1
            )
            moved = jnp.dot(around, shift_ref[...], preferred_element_type=F32)
            for slot in range(SLOTS):
                for half in range(2):
                    begin = CB * slot + 128 * half
                    mixed_ref[2 * part + half, pl.ds(slot, CB, stride=SLOTS), :] = moved[:, begin : begin + 128]
            for half in range(2):
                there = pl.ds(pl.multiple_of(d * CB + 128 * half, 128), 128)
                lhs_ref[:, there] = mixed_ref[2 * part + half].astype(BF16)

    def shift_first():
        inner = (y // 2) * 4 + 1
        shift(inner, inner + 1)

    def shift_rest():
        inner = (1 - y // 2) * 4 + 1

        def step(index, carry):
            first = jnp.where(index == 0, inner, jnp.where(index == 1, 3, 0))
            second = jnp.where(index == 0, inner + 1, jnp.where(index == 1, 4, 7))
            shift(first, second)
            return carry

        lax.fori_loop(0, 3, step, 0)

    def act(actions):
        for kind, what in actions:
            if kind == "w":
                block_wait(what)
            elif kind == "s":
                block_copy(what).start()
            elif kind == "y":
                hand_over(what)
                if what in ((0, 0), (2, 0)):
                    turn(what)
                if what == (0, 0):
                    shift_first()
            elif kind == "L":
                shift_rest()
            elif kind == "D":
                taken_over(what)

    spans, span = [], []
    for action in ACTIONS:
        span.append(action)
        if action[0] in ("C", "D"):
            spans.append(span)
            span = []

    act(spans[0])

    def product(index, carry):
        for number in range(1, len(spans)):
            pl.when(index == number)(functools.partial(act, spans[number]))
        group, other = pick(PRODUCTS, index)
        part_ref[index] = multiply(lhs_ref, g_ref, group_channels(coords, group, other))
        return carry

    lax.fori_loop(0, EARLY, product, 0)
    act(span)
    for group, other in LATE:
        if other:
            taken_over(group)

    for step in range(1, 8):
        stat_copy(step).wait_send()
    gone = g_ref.at[pl.ds(0, 63)]
    pltpu.make_async_copy(gone, gone, send_sem).wait()
    gone = g_ref.at[pl.ds(0, 64)]
    pltpu.make_async_copy(gone, gone, other_send).wait()


def finish_kernel(part_ref, lhs_ref, g_ref, out_ref, stage_ref, part_sem, stage_sem):
    coords = dims()

    def columns(group, other):
        channels = group_channels(coords, group, other)
        return out_ref.at[:, :, pl.ds(pl.multiple_of(channels * CB, CB), CB)]

    def early_copy(index):
        return pltpu.make_async_copy(part_ref.at[index], columns(*pick(PRODUCTS, index)), part_sem.at[index])

    def late_copy(index):
        return pltpu.make_async_copy(stage_ref.at[index], columns(*pick(LATE, index)), stage_sem.at[index])

    def early(index, carry):
        early_copy(index).start()
        return carry

    def late(index, carry):
        stage_ref[index] = multiply(lhs_ref, g_ref, group_channels(coords, *pick(LATE, index)))
        late_copy(index).start()
        return carry

    def early_end(index, carry):
        early_copy(index).wait()
        return carry

    def late_end(index, carry):
        late_copy(index).wait()
        return carry

    lax.fori_loop(0, EARLY, early, 0)
    lax.fori_loop(0, len(LATE), late, 0)
    lax.fori_loop(0, EARLY, early_end, 0)
    lax.fori_loop(0, len(LATE), late_end, 0)


def local(raw, fir_taps, channel_map, lag_offsets):
    vmem = pl.BlockSpec(memory_space=pltpu.VMEM)
    given = (raw.T, fir_taps.reshape(1, TAPS), channel_map.reshape(1, CB), lag_offsets.reshape(1, SLOTS))
    hbm = pl.BlockSpec(memory_space=pltpu.HBM)
    part, lhs, blocks = pl.pallas_call(
        gather_kernel,
        out_shape=[
            pltpu.VMEM((EARLY, CB, SLOTS, CB), F32),
            pltpu.VMEM((CB * SLOTS, 8 * CB), BF16),
            pltpu.VMEM((128, CB, CB), BF16),
        ],
        in_specs=[hbm] * 4,
        out_specs=[vmem] * 3,
        scratch_shapes=[
            pltpu.VMEM((ROWS, CB), BF16),
            pltpu.VMEM((1, TAPS), BF16),
            pltpu.VMEM((1, CB), jnp.int32),
            pltpu.VMEM((1, SLOTS), jnp.int32),
            pltpu.VMEM((CB, CB), F32),
            pltpu.VMEM((8, 8, CB), F32),
            pltpu.VMEM((10, CB, CB), BF16),
            pltpu.VMEM((512, SLOTS * CB), BF16),
            pltpu.VMEM((4, CB * SLOTS, 128), F32),
            pltpu.SemaphoreType.DMA((4,)),
            pltpu.SemaphoreType.DMA((3,)),
            pltpu.SemaphoreType.DMA((8,)),
            pltpu.SemaphoreType.DMA((8,)),
            pltpu.SemaphoreType.DMA,
            pltpu.SemaphoreType.DMA((len(COPIES),)),
            pltpu.SemaphoreType.DMA,
            pltpu.SemaphoreType.DMA((16,)),
        ],
        compiler_params=pltpu.CompilerParams(collective_id=0, has_side_effects=True, vmem_limit_bytes=14 << 20),
        name="gather",
    )(*[pltpu.with_memory_space_constraint(a, pltpu.HBM) for a in given])
    part, lhs, blocks = [pltpu.with_memory_space_constraint(a, pltpu.VMEM) for a in (part, lhs, blocks)]
    return pl.pallas_call(
        finish_kernel,
        out_shape=jax.ShapeDtypeStruct((CB, SLOTS, CHANNELS), F32),
        in_specs=[vmem] * 3,
        out_specs=pl.BlockSpec(memory_space=pltpu.HBM),
        scratch_shapes=[
            pltpu.VMEM((len(LATE), CB, SLOTS, CB), F32),
            pltpu.SemaphoreType.DMA((EARLY,)),
            pltpu.SemaphoreType.DMA((len(LATE),)),
        ],
        compiler_params=pltpu.CompilerParams(vmem_limit_bytes=(len(LATE) + 3) << 20),
        name="finish",
    )(part, lhs, blocks)


def solution(mesh):
    placed = (P("chan", "lag"), P(), P("chan"), P("lag"))
    return jax.shard_map(
        local, mesh=mesh, in_specs=placed, out_specs=P("chan", "lag", None), check_vma=False
    )
```

```python
import functools
import math

import jax
import jax.numpy as jnp
from jax import lax
from jax.experimental import pallas as pl
from jax.experimental.pallas import tpu as pltpu
from jax.sharding import PartitionSpec as P

MESH = pl.DeviceIdType.MESH
DEC = 20
TAPS = 80
MAXLAG = 40
CB = 256
SAMPLES = 2000
CHANNELS = 4096
SLOTS = 4
STEP = 250
HEAD = 3
ROWS = 5000
F32, BF16 = jnp.float32, jnp.bfloat16

COPIES = (
    ((0, 0, 1), 2, 0, 80), ((0, 0, 1), 2, 80, 80), ((0, 0, 1), 2, 160, 96), ((0, 0, 2), 2, 0, 256),
    ((0, 0, 3), 2, 0, 80), ((0, 0, 3), 2, 80, 80), ((0, 0, 3), 2, 160, 96), ((0, 1, 0), 1, 0, 80),
    ((0, 1, 0), 1, 80, 80), ((0, 1, 0), 1, 160, 96), ((0, 1, 1), 2, 0, 256), ((0, 1, 2), 2, 0, 256),
    ((0, 1, 3), 2, 0, 256), ((0, 2, 0), 1, 0, 256), ((0, 2, 1), 1, 0, 256), ((0, 2, 2), 1, 0, 256),
    ((0, 2, 3), 2, 0, 256), ((0, 3, 0), 1, 0, 80), ((0, 3, 0), 1, 80, 80), ((0, 3, 0), 1, 160, 96),
    ((0, 3, 1), 1, 0, 80), ((0, 3, 1), 2, 80, 176), ((0, 3, 2), 1, 0, 256), ((0, 3, 3), 2, 0, 256),
    ((1, 0, 0), 0, 0, 80), ((1, 0, 0), 0, 80, 80), ((1, 0, 0), 0, 160, 96), ((1, 0, 1), 2, 0, 256),
    ((1, 0, 2), 2, 0, 256), ((1, 0, 3), 0, 0, 80), ((1, 0, 3), 2, 80, 176), ((1, 1, 0), 1, 0, 160),
    ((1, 1, 0), 0, 160, 96), ((1, 1, 1), 0, 0, 256), ((1, 1, 2), 0, 0, 256), ((1, 1, 3), 1, 0, 256),
    ((1, 2, 0), 1, 0, 80), ((1, 2, 0), 0, 80, 176), ((1, 2, 1), 0, 0, 256), ((1, 2, 2), 0, 0, 256),
    ((1, 2, 3), 1, 0, 256), ((1, 3, 0), 1, 0, 256), ((1, 3, 1), 1, 0, 80), ((1, 3, 1), 1, 160, 96),
    ((1, 3, 1), 2, 80, 80), ((1, 3, 2), 1, 0, 256), ((1, 3, 3), 1, 0, 256), ((2, 0, 0), 0, 0, 256),
    ((2, 0, 1), 2, 0, 80), ((2, 0, 1), 0, 80, 176), ((2, 0, 2), 2, 0, 256), ((2, 0, 3), 0, 0, 256),
    ((2, 1, 0), 0, 0, 256), ((2, 1, 1), 2, 0, 256), ((2, 1, 2), 2, 0, 256), ((2, 1, 3), 2, 0, 256),
    ((2, 2, 0), 1, 0, 80), ((2, 2, 0), 0, 80, 176), ((2, 2, 1), 1, 0, 256), ((2, 2, 2), 2, 0, 256),
    ((2, 2, 3), 1, 0, 256), ((2, 3, 0), 0, 0, 80), ((2, 3, 0), 1, 80, 176), ((2, 3, 1), 1, 0, 256),
    ((2, 3, 2), 2, 0, 256), ((2, 3, 3), 1, 0, 256), ((3, 0, 0), 0, 0, 80), ((3, 0, 0), 0, 80, 80),
    ((3, 0, 0), 0, 160, 96), ((3, 0, 1), 2, 0, 160), ((3, 0, 1), 0, 160, 96), ((3, 0, 2), 2, 0, 256),
    ((3, 0, 3), 0, 0, 160), ((3, 0, 3), 2, 160, 96), ((3, 1, 0), 1, 0, 256), ((3, 1, 1), 0, 0, 256),
    ((3, 1, 2), 1, 0, 256), ((3, 1, 3), 0, 0, 256), ((3, 2, 0), 1, 0, 160), ((3, 2, 0), 0, 160, 96),
    ((3, 2, 1), 0, 0, 256), ((3, 2, 2), 0, 0, 256), ((3, 2, 3), 2, 0, 256), ((3, 3, 0), 0, 0, 80),
    ((3, 3, 0), 0, 160, 96), ((3, 3, 0), 1, 80, 80), ((3, 3, 1), 2, 0, 256), ((3, 3, 2), 0, 0, 256),
    ((3, 3, 3), 2, 0, 256),
)
ACTIONS = (
    ("s", 67), ("s", 17), ("s", 2), ("s", 66), ("s", 18), ("s", 0), ("s", 68), ("s", 19), ("s", 4), ("s", 24),
    ("s", 9), ("s", 5), ("s", 25), ("s", 7), ("s", 6), ("s", 26), ("s", 8), ("s", 1), ("w", 67), ("s", 85),
    ("w", 17), ("s", 83), ("w", 2), ("s", 70), ("w", 66), ("s", 69), ("w", 0), ("s", 20), ("w", 68), ("s", 47),
    ("w", 18), ("w", 19), ("s", 13), ("s", 21), ("s", 84), ("s", 74), ("s", 73), ("w", 4), ("s", 29), ("s", 23),
    ("w", 5), ("s", 72), ("w", 9), ("s", 32), ("w", 24), ("w", 25), ("s", 31), ("w", 6), ("s", 3), ("w", 26),
    ("s", 41), ("s", 30), ("w", 8), ("w", 7), ("s", 10), ("s", 27), ("s", 12), ("w", 83), ("s", 61), ("w", 85),
    ("s", 78), ("w", 69), ("w", 70), ("s", 49), ("w", 20), ("w", 21), ("s", 14), ("w", 47), ("s", 62), ("s", 48),
    ("w", 13), ("s", 79), ("s", 16), ("s", 37), ("y", (0, 0)), ("w", 74), ("s", 52), ("w", 84), ("s", 86),
    ("w", 72), ("w", 73), ("s", 51), ("s", 88), ("w", 61), ("s", 56), ("w", 3), ("s", 22), ("s", 71), ("w", 41),
    ("s", 36), ("w", 29), ("w", 30), ("s", 46), ("s", 35), ("w", 78), ("w", 79), ("s", 57), ("s", 44), ("s", 82),
    ("w", 10), ("s", 33), ("s", 75), ("w", 14), ("s", 38), ("s", 80), ("s", 28), ("w", 27), ("s", 42), ("s", 43),
    ("w", 62), ("y", (3, 0)), ("w", 31), ("w", 32), ("w", 52), ("y", (1, 0)), ("s", 53), ("w", 12), ("s", 77),
    ("w", 51), ("s", 65), ("y", (0, 3)), ("w", 48), ("w", 49), ("s", 63), ("w", 22), ("s", 87), ("s", 15),
    ("s", 55), ("w", 1), ("y", (0, 1)), ("w", 36), ("w", 37), ("w", 56), ("w", 57), ("y", (2, 0)), ("L", 0),
    ("w", 46), ("s", 40), ("s", 11), ("s", 50), ("C", 1), ("w", 65), ("s", 60), ("s", 64), ("w", 71), ("s", 76),
    ("w", 23), ("w", 88), ("y", (3, 3)), ("D", 1), ("w", 63), ("s", 58), ("w", 42), ("w", 43), ("w", 44), ("w", 86),
    ("y", (3, 1)), ("w", 15), ("s", 39), ("s", 81), ("C", 0), ("w", 28), ("s", 45), ("D", 0), ("w", 60), ("s", 59),
    ("w", 55), ("s", 54), ("w", 33), ("w", 53), ("w", 75), ("y", (1, 1)), ("w", 16), ("w", 40), ("w", 82),
    ("y", (2, 3)), ("w", 35), ("w", 77), ("y", (1, 3)), ("C", 3), ("w", 11), ("s", 34), ("C", 4), ("w", 38),
    ("w", 58), ("w", 80), ("y", (2, 1)), ("w", 50), ("y", (0, 2)), ("C", 5), ("w", 45), ("w", 64), ("w", 87),
    ("y", (3, 2)), ("D", 3), ("w", 39), ("w", 59), ("w", 81), ("y", (2, 2)), ("D", 4), ("w", 34), ("w", 54),
    ("w", 76), ("y", (1, 2)), ("D", 5), ("C", 2),
)

PRODUCTS = [(what, int(kind == "D")) for kind, what in ACTIONS if kind in ("C", "D")]
LATE = [(group, other) for group in range(8) for other in range(2) if (group, other) not in PRODUCTS]
EARLY = len(PRODUCTS)


def digits(values, bits):
    return sum(value << (bits * index) for index, value in enumerate(values))


def digit(packed, index, bits):
    return lax.shift_right_logical(jnp.int32(packed), index * bits) & ((1 << bits) - 1)


def pick(products, index):
    group = digit(digits([g % 2 for g, _ in products], 1), index, 1)
    group += 2 * digit(digits([g // 2 for g, _ in products], 2), index, 2)
    return group, digit(digits([o for _, o in products], 1), index, 1)


def dims():
    chan, lag = lax.axis_index("chan"), lax.axis_index("lag")
    core, z, y_lo = chan % 2, (chan // 2) % 4, chan // 8
    x, y = lag % 4, (lag // 4) * 2 + y_lo
    return x, y, z, core


def device(x, y, z, core):
    return (((y % 2) * 4 + z) * 2 + core, (y // 2) * 4 + x)


def group_channels(coords, group, other):
    _, y, z, core = coords
    sign = (1 - 2 * core) * (1 - 2 * other)
    step = group // 2
    step = step + (step // 2) * (5 - 2 * step)
    z_there = (z + 4 + sign * (step - 4 * (step // 3))) % 4
    core_there = core + other - 2 * core * other
    return (((y + group) % 2) * 4 + z_there) * 2 + core_there


def multiply(lhs_ref, g_ref, channels):
    block = g_ref[pl.ds(channels * 8, 8)].reshape(8 * CB, CB)
    product = jnp.dot(lhs_ref[...], block, preferred_element_type=F32)
    return (product * (1.0 / math.sqrt(SAMPLES))).reshape(CB, SLOTS, CB)


def gather_kernel(
    raw_hbm, taps_hbm, map_hbm, lags_hbm, part_ref, lhs_ref, g_ref,
    raw_ref, taps_ref, map_ref, lags_ref, dec_ref, stat_ref, turned_ref, shift_ref, mixed_ref,
    raw_sem, small_sem, stat_send, stat_recv, send_sem, recv_sem, other_send, other_recv,
):
    coords = x, y, z, core = dims()
    me, lag = device(*coords)
    ahead = 1 - 2 * core

    small_copies = [
        pltpu.make_async_copy(there, here, small_sem.at[index])
        for index, (there, here) in enumerate(((taps_hbm, taps_ref), (lags_hbm, lags_ref), (map_hbm, map_ref)))
    ]
    for copy in small_copies:
        copy.start()
    raw_copies = []
    for index in range(4):
        rows = pl.ds(1280 * index, min(1280, ROWS - 1280 * index))
        raw_copies.append(pltpu.make_async_copy(raw_hbm.at[rows], raw_ref.at[rows], raw_sem.at[index]))
        raw_copies[-1].start()

    def lag_peer(step):
        return me, (lag + step) % 8

    sibling = device(x, y, z, 1 - core)
    barrier = pltpu.get_barrier_semaphore()
    peers = [lag_peer(step) for step in range(1, 8)] + [sibling]
    peers += [device(x, (y + step) % 4, z, core) for step in (1, 3)]
    peers += [device(x, y, (z + step) % 4, core) for step in (1, 2, 3)]
    for peer in peers:
        pl.semaphore_signal(barrier, inc=1, device_id=peer, device_id_type=MESH)

    small_copies[0].wait()
    taps = jnp.broadcast_to(taps_ref[...].astype(F32), (8, TAPS)).astype(BF16)
    spread = lax.broadcasted_iota(jnp.int32, (TAPS, 256), 0) + lax.broadcasted_iota(jnp.int32, (TAPS, 256), 1)
    spread = (spread == 128 + DEC - 1).astype(F32).astype(BF16)
    first = jnp.dot(taps, spread, preferred_element_type=F32)
    first = jnp.concatenate([first, jnp.zeros((8, 512), F32)], axis=1)
    wide = lax.broadcasted_iota(jnp.int32, (8, 768), 0)
    band = first
    for step in range(1, 8):
        band = jnp.where(wide == step, pltpu.roll(first, DEC * step, 1), band)
    band = jnp.concatenate([band] + [pltpu.roll(band, 8 * DEC * step, 1) for step in range(1, 4)], axis=0)
    next_band = pltpu.roll(band[0:16, 0:256], 8, 1).astype(BF16)
    band = band.astype(BF16)

    def tail():
        last = raw_ref[4992:5000].astype(F32)
        last = jnp.concatenate([last, jnp.zeros((8, CB), F32)], axis=0).astype(BF16)
        return [last, jnp.zeros((112, CB), BF16)]

    for part in range(8):
        begin = 640 * part - 128
        if part % 2 == 0:
            raw_copies[part // 2].wait()
        if part == 0:
            piece = jnp.dot(band[:, 128:], raw_ref[0:640], preferred_element_type=F32)
        elif part == 7:
            window = jnp.concatenate([raw_ref[begin:4992]] + tail(), axis=0)
            piece = jnp.dot(band, window, preferred_element_type=F32)
        else:
            piece = jnp.dot(band, raw_ref[begin : begin + 768], preferred_element_type=F32)
        dec_ref[32 * part : 32 * part + 32] = piece
    window = jnp.concatenate([raw_ref[4864:4992]] + tail(), axis=0)
    over = jnp.dot(next_band, window, preferred_element_type=F32)[0:8]

    dec = dec_ref[...]
    sample = lax.broadcasted_iota(jnp.int32, (CB, CB), 0)
    whole = (sample >= HEAD) & (sample < STEP)
    count = STEP - HEAD
    mean = jnp.sum(jnp.where(whole, dec, 0.0), axis=0, keepdims=True) * (1.0 / count)
    spread2 = jnp.where(whole, dec - mean, 0.0)
    energy = jnp.sum(spread2 * spread2, axis=0, keepdims=True)
    line = lax.broadcasted_iota(jnp.int32, (8, CB), 0)
    stat_ref[lag] = jnp.where(
        line == 0,
        mean,
        jnp.where(
            line == 1,
            energy,
            jnp.where(line < 5, pltpu.roll(dec[0:8], 2, 0), pltpu.roll(over, 5, 0)),
        ),
    )
    pl.semaphore_wait(barrier, len(peers))

    def stat_copy(step):
        return pltpu.make_async_remote_copy(
            src_ref=stat_ref.at[lag],
            dst_ref=stat_ref.at[lag],
            send_sem=stat_send.at[step],
            recv_sem=stat_recv.at[step],
            device_id=lag_peer(step),
            device_id_type=MESH,
        )

    for step in range(1, 8):
        stat_copy(step).start()
    row = lax.broadcasted_iota(jnp.int32, (512, 256), 0)
    far = 10000
    time = jnp.where(
        row < 256,
        jnp.where(row < STEP, row, far),
        jnp.where(row < 384, jnp.where(row - 128 < STEP, row - 128 - STEP, far), row - 384 + STEP),
    )
    column = lax.broadcasted_iota(jnp.int32, (512, 256), 1)
    column = jnp.where(column < STEP, column, -far)
    time = time - column
    small_copies[1].wait()
    for slot in range(SLOTS):
        shift_ref[:, CB * slot : CB * slot + CB] = (time == -lags_ref[0:1, slot : slot + 1]).astype(F32).astype(BF16)

    order = lax.broadcasted_iota(jnp.int32, (CB, CB), 0)
    small_copies[2].wait()
    place = (map_ref[...] - (me * CB) == order).astype(F32).astype(BF16)
    for step in range(1, 8):
        stat_copy(step).wait_recv()

    stats = [stat_ref[d] for d in range(8)]
    total = jnp.zeros((8, CB), F32)
    heads = []
    before = jnp.zeros((8, CB), F32)
    for d in range(8):
        head = pltpu.roll(stats[d], 6, 0)
        if d:
            from_left = pltpu.roll(stats[d - 1], 3, 0)
            head = head + from_left
            before = before + jnp.where(lag == d, from_left, 0.0)
        heads.append(head)
        total = total + jnp.where(line < HEAD, head, 0.0)
    mean = count * sum(s[0:1] for s in stats) + jnp.sum(total, axis=0, keepdims=True)
    mean = mean * (1.0 / SAMPLES)
    energy = jnp.zeros((1, CB), F32)
    total = jnp.zeros((8, CB), F32)
    for d in range(8):
        away = stats[d][0:1] - mean
        energy = energy + stats[d][1:2] + count * (away * away)
        away = jnp.where(line < HEAD, heads[d] - mean, 0.0)
        total = total + away * away
    energy = (energy + jnp.sum(total, axis=0, keepdims=True)) * (1.0 / SAMPLES)
    scale = lax.rsqrt(energy + 1e-05)
    dec_ref[0:8] = dec_ref[0:8] + jnp.where(line < HEAD, before, 0.0)
    white = jnp.where(sample < STEP, (dec_ref[...] - mean) * scale, 0.0).astype(BF16)
    ordered = lax.dot_general(white, place, (((1,), (1,)), ((), ())), preferred_element_type=F32)

    there = (0, 1, 2, -1)
    at_x = [(x + 4 + ahead * k) % 4 for k in there]
    at_y = [(y + 4 + ahead * k) % 4 for k in there]
    at_z = [(z + 4 + ahead * k) % 4 for k in there]
    term_y = [(k % 2) * 64 + (k // 2) * 4 for k in at_y]
    term_z = [k * 16 + core * 8 for k in at_z]

    def place_of(offset):
        return at_x[offset[0]] + term_y[offset[1]] + term_z[offset[2]]

    neighbours = {}
    for step in (1, 2, 3):
        neighbours[0, step] = device(at_x[step], y, z, core)
        neighbours[1, step] = device(x, at_y[step], z, core)
        neighbours[2, step] = device(x, y, at_z[step], core)

    g_ref[place_of((0, 0, 0))] = ordered.astype(BF16)
    turned_ref[0] = jnp.zeros((CB, CB), BF16)
    turned_ref[9] = jnp.zeros((CB, CB), BF16)

    def block_copy(index):
        offset, axis, row, rows = COPIES[index]
        axis, far = axis % 3, axis // 3
        sent = list(offset)
        sent[axis] = {1: 0, 3: 0, 2: 0 if far else 3}[offset[axis]]
        to = 2 if far else 3 if offset[axis] == 1 else 1
        here = g_ref.at[place_of(sent), pl.ds(row, rows)]
        return pltpu.make_async_remote_copy(
            src_ref=here, dst_ref=here, send_sem=send_sem, recv_sem=recv_sem.at[index],
            device_id=neighbours[axis, to], device_id_type=MESH,
        )

    def block_wait(index):
        offset, axis, row, rows = COPIES[index]
        here = g_ref.at[place_of(offset), pl.ds(row, rows)]
        pltpu.make_async_copy(here, here, recv_sem.at[index]).wait()

    def line_of(offset):
        return pl.ds(term_y[offset[0]] + term_z[offset[1]], 4)

    def hand_over(offset):
        here = g_ref.at[line_of(offset)]
        half = (at_y[offset[0]] % 2) * 4 + at_z[offset[1]] + 8 * (at_y[offset[0]] // 2)
        pltpu.make_async_remote_copy(
            src_ref=here, dst_ref=here, send_sem=other_send, recv_sem=other_recv.at[half],
            device_id=sibling, device_id_type=MESH,
        ).start()

    def taken_over(group):
        channels = group_channels(coords, group, True)
        for half in range(2):
            here = g_ref.at[pl.ds(channels * 8 + 4 * half, 4)]
            pltpu.make_async_copy(here, here, other_recv.at[channels // 2 + 8 * half]).wait()

    eye = lax.broadcasted_iota(jnp.int32, (CB, CB), 0) == lax.broadcasted_iota(jnp.int32, (CB, CB), 1)
    eye = eye.astype(F32).astype(BF16)

    def turn(offset):
        first = (at_y[offset[0]] // 2) * 4
        for part in range(4):
            block = g_ref[me * 8 + first + part]
            turned = lax.dot_general(eye, block, (((1,), (1,)), ((), ())), preferred_element_type=F32)
            turned_ref[first + part + 1] = turned.astype(BF16)

    def shift(*pair):
        for part, d in enumerate(pair):
            around = jnp.concatenate(
                [turned_ref[d + 1], turned_ref[d, :, 128:256], turned_ref[d + 2, :, 0:128]], axis=1
            )
            moved = jnp.dot(around, shift_ref[...], preferred_element_type=F32)
            for slot in range(SLOTS):
                for half in range(2):
                    begin = CB * slot + 128 * half
                    mixed_ref[2 * part + half, pl.ds(slot, CB, stride=SLOTS), :] = moved[:, begin : begin + 128]
            for half in range(2):
                there = pl.ds(pl.multiple_of(d * CB + 128 * half, 128), 128)
                lhs_ref[:, there] = mixed_ref[2 * part + half].astype(BF16)

    def shift_first():
        inner = (y // 2) * 4 + 1
        shift(inner, inner + 1)

    def shift_rest():
        inner = (1 - y // 2) * 4 + 1

        def step(index, carry):
            first = jnp.where(index == 0, inner, jnp.where(index == 1, 3, 0))
            second = jnp.where(index == 0, inner + 1, jnp.where(index == 1, 4, 7))
            shift(first, second)
            return carry

        lax.fori_loop(0, 3, step, 0)

    def act(actions):
        for kind, what in actions:
            if kind == "w":
                block_wait(what)
            elif kind == "s":
                block_copy(what).start()
            elif kind == "y":
                hand_over(what)
                if what in ((0, 0), (2, 0)):
                    turn(what)
                if what == (0, 0):
                    shift_first()
            elif kind == "L":
                shift_rest()
            elif kind == "D":
                taken_over(what)

    spans, span = [], []
    for action in ACTIONS:
        span.append(action)
        if action[0] in ("C", "D"):
            spans.append(span)
            span = []

    act(spans[0])

    def product(index, carry):
        for number in range(1, len(spans)):
            pl.when(index == number)(functools.partial(act, spans[number]))
        group, other = pick(PRODUCTS, index)
        part_ref[index] = multiply(lhs_ref, g_ref, group_channels(coords, group, other))
        return carry

    lax.fori_loop(0, EARLY, product, 0)
    act(span)
    for group, other in LATE:
        if other:
            taken_over(group)

    for step in range(1, 8):
        stat_copy(step).wait_send()
    gone = g_ref.at[pl.ds(0, 63)]
    pltpu.make_async_copy(gone, gone, send_sem).wait()
    gone = g_ref.at[pl.ds(0, 64)]
    pltpu.make_async_copy(gone, gone, other_send).wait()


def finish_kernel(part_ref, lhs_ref, g_ref, out_ref, stage_ref, part_sem, stage_sem):
    coords = dims()

    def columns(group, other):
        channels = group_channels(coords, group, other)
        return out_ref.at[:, :, pl.ds(pl.multiple_of(channels * CB, CB), CB)]

    def early_copy(index):
        return pltpu.make_async_copy(part_ref.at[index], columns(*pick(PRODUCTS, index)), part_sem.at[index])

    def late_copy(index):
        return pltpu.make_async_copy(stage_ref.at[index], columns(*pick(LATE, index)), stage_sem.at[index])

    def early(index, carry):
        early_copy(index).start()
        return carry

    def late(index, carry):
        stage_ref[index] = multiply(lhs_ref, g_ref, group_channels(coords, *pick(LATE, index)))
        late_copy(index).start()
        return carry

    def early_end(index, carry):
        early_copy(index).wait()
        return carry

    def late_end(index, carry):
        late_copy(index).wait()
        return carry

    lax.fori_loop(0, EARLY, early, 0)
    lax.fori_loop(0, len(LATE), late, 0)
    lax.fori_loop(0, EARLY, early_end, 0)
    lax.fori_loop(0, len(LATE), late_end, 0)


def local(raw, fir_taps, channel_map, lag_offsets):
    vmem = pl.BlockSpec(memory_space=pltpu.VMEM)
    given = (raw.T, fir_taps.reshape(1, TAPS), channel_map.reshape(1, CB), lag_offsets.reshape(1, SLOTS))
    hbm = pl.BlockSpec(memory_space=pltpu.HBM)
    part, lhs, blocks = pl.pallas_call(
        gather_kernel,
        out_shape=[
            pltpu.VMEM((EARLY, CB, SLOTS, CB), F32),
            pltpu.VMEM((CB * SLOTS, 8 * CB), BF16),
            pltpu.VMEM((128, CB, CB), BF16),
        ],
        in_specs=[hbm] * 4,
        out_specs=[vmem] * 3,
        scratch_shapes=[
            pltpu.VMEM((ROWS, CB), BF16),
            pltpu.VMEM((1, TAPS), BF16),
            pltpu.VMEM((1, CB), jnp.int32),
            pltpu.VMEM((1, SLOTS), jnp.int32),
            pltpu.VMEM((CB, CB), F32),
            pltpu.VMEM((8, 8, CB), F32),
            pltpu.VMEM((10, CB, CB), BF16),
            pltpu.VMEM((512, SLOTS * CB), BF16),
            pltpu.VMEM((4, CB * SLOTS, 128), F32),
            pltpu.SemaphoreType.DMA((4,)),
            pltpu.SemaphoreType.DMA((3,)),
            pltpu.SemaphoreType.DMA((8,)),
            pltpu.SemaphoreType.DMA((8,)),
            pltpu.SemaphoreType.DMA,
            pltpu.SemaphoreType.DMA((len(COPIES),)),
            pltpu.SemaphoreType.DMA,
            pltpu.SemaphoreType.DMA((16,)),
        ],
        compiler_params=pltpu.CompilerParams(collective_id=0, has_side_effects=True, vmem_limit_bytes=14 << 20),
        name="gather",
    )(*[pltpu.with_memory_space_constraint(a, pltpu.HBM) for a in given])
    part, lhs, blocks = [pltpu.with_memory_space_constraint(a, pltpu.VMEM) for a in (part, lhs, blocks)]
    return pl.pallas_call(
        finish_kernel,
        out_shape=jax.ShapeDtypeStruct((CB, SLOTS, CHANNELS), F32),
        in_specs=[vmem] * 3,
        out_specs=pl.BlockSpec(memory_space=pltpu.HBM),
        scratch_shapes=[
            pltpu.VMEM((len(LATE), CB, SLOTS, CB), F32),
            pltpu.SemaphoreType.DMA((EARLY,)),
            pltpu.SemaphoreType.DMA((len(LATE),)),
        ],
        compiler_params=pltpu.CompilerParams(vmem_limit_bytes=(len(LATE) + 3) << 20),
        name="finish",
    )(part, lhs, blocks)


def solution(mesh):
    placed = (P("chan", "lag"), P(), P("chan"), P("lag"))
    return jax.shard_map(
        local, mesh=mesh, in_specs=placed, out_specs=P("chan", "lag", None), check_vma=False
    )
```
